512 devices in a mesh: section: 32 (over z_lo, y), dp: 16 (over z_hi, x, core).
Axes of the slice: x: 4, y: 8, z: 8 (z_hi: 2, z_lo: 4; z = z_hi * 4 + z_lo), core: 2. Of those that a mesh axis runs over, the one named last changes fastest.
Arguments:
- section_inputs: bfloat16 [32, 4096, 4096], P('section', 'dp'), may hold values from -6 to 6
- grad_first: bfloat16 [32, 1024, 4096], P('section', 'dp'), may hold values from -6 to 6
- value_master: float32 [32, 4096, 512], P('section', 'dp'), may hold values from -4 to 4
- first_moment: bfloat16 [32, 4096, 512], P('section', 'dp'), may hold values from -3 to 3
- second_moment: bfloat16 [32, 4096, 512], P('section', 'dp'), may hold values from 0.099609375 to 10
- output_weight: bfloat16 [32, 512, 4096], P('section', None, 'dp'), may hold values from -0.25 to 0.25
Outputs:
- master_next: float32 [32, 4096, 512], P('section', 'dp')
- first_next: bfloat16 [32, 4096, 512], P('section', 'dp')
- second_next: bfloat16 [32, 4096, 512], P('section', 'dp')
The draws below stay inside these ranges and needn't reach their ends.
All inputs are finite; a program needn't handle non-finite values.
Results may differ from the reference program's by a relative error of at most 0.012.
Values may be sent and summed in bfloat16 or wider, within the bound.
A program may use at most 64 MiB of HBM per device.

```python
import math
import jax
import jax.numpy as jnp
from jax import lax

D = 4096
R = 512
MB = 64
MICRO = 4
SECTIONS = 32
TOKENS = 4096
ROWS = 1024
N_DP = 16


def strengthened(array, own_key, source, target, shards_of, factor):
    def block_of(dim):
        return (jnp.arange(array.shape[dim]) // (array.shape[dim] // shards_of)).reshape((-1,) + (1,) * (array.ndim - 1 - dim))

    near = jax.random.permutation(own_key, shards_of)[block_of(target)]
    other_side = (block_of(target) + shards_of // 2) % shards_of
    return jnp.where((block_of(source) == near) | (block_of(source) == other_side), factor * array, array)


def levels(own_key, extent, pieces, low, largest):
    def one(axis_at, blocks):
        heights = jax.random.uniform(jax.random.fold_in(jax.random.fold_in(own_key, 6), axis_at), (blocks,), jnp.float32, low / len(pieces), largest / len(pieces))
        return jnp.repeat(jnp.exp(heights), extent[axis_at] // blocks).reshape((-1,) + (1,) * (len(extent) - axis_at - 1))

    level = one(*pieces[0])
    for cut in pieces[1:]:
        level = level * one(*cut)
    return level


def bell_draw(key, dims, width, bound, shards=(), held_as=jnp.bfloat16):
    factor_of = levels(key, dims, shards, -0.22, 0.18) if shards else 1.0
    entries = jax.random.normal(key, dims, jnp.float32) * width * factor_of
    return jnp.minimum(jnp.maximum(entries, -bound), bound).astype(held_as)


def gaussian_with(rng, dims, spread, limit, cuts, heavy, kind=jnp.bfloat16):
    array = spread * jax.random.normal(rng, dims, jnp.float32)
    if cuts:
        array = array * levels(rng, dims, cuts, -0.22, 0.18)
    return jnp.clip(strengthened(array, jax.random.fold_in(rng, 3), *heavy), -limit, limit).astype(kind)


def setup_inputs(seed: int = 0) -> dict:
    streams_of = jax.random.split(jax.random.key(seed), 7)
    return {
        "section_inputs": gaussian_with(streams_of[0], (SECTIONS, TOKENS, D), 1.0, 6.0, ((0, 32), (1, 16)), (1, 2, 16, 2.0)),
        "grad_first": bell_draw(streams_of[1], (SECTIONS, ROWS, D), 1.0, 6.0, ((0, 32), (1, 16))),
        "value_master": bell_draw(streams_of[2], (SECTIONS, D, R), 1.0, 4.0, ((0, 32), (1, 16)), jnp.float32),
        "first_moment": bell_draw(streams_of[3], (SECTIONS, D, R), 0.5, 3.0, ((0, 32), (1, 16))),
        "second_moment": jnp.clip(jnp.exp(math.log(10.0) - 4.609084 * jax.random.uniform(streams_of[4], (SECTIONS, D, R), jnp.float32) ** levels(streams_of[4], (SECTIONS, D, R), ((0, 32), (1, 16)), -0.2, 0.2)), 0.099609375, 10.0).astype(jnp.bfloat16),
        "output_weight": bell_draw(streams_of[5], (SECTIONS, R, D), R ** -0.5, 0.25, ((0, 32), (2, 16))),
    }


def section_backward(x, g, master, out_w):
    scale = 1.0 / math.sqrt(D)
    weight = master.astype(jnp.bfloat16)
    xf = x.astype(jnp.float32)
    rinv = lax.rsqrt(lax.optimization_barrier(jnp.mean(xf * xf, axis=-1, keepdims=True)) + 1e-05)
    normed = xf * rinv
    hidden = normed.astype(jnp.bfloat16)
    upper = jnp.dot(hidden, weight, preferred_element_type=jnp.float32) * scale
    back = jnp.dot(g, out_w.T, preferred_element_type=jnp.float32)
    sig = jax.nn.sigmoid(upper)
    delta = (back * sig * (1.0 + upper * (1.0 - sig))).astype(jnp.bfloat16)
    dh = jnp.dot(delta, weight.T, preferred_element_type=jnp.float32) * scale
    dx = g.astype(jnp.float32) + rinv * (dh - normed * lax.optimization_barrier(jnp.mean(normed * dh, axis=-1, keepdims=True)))
    return (delta, dx.astype(jnp.bfloat16))

def section_update(args):
    x, deltas, master, first, second = args
    scale = 1.0 / math.sqrt(D)
    xf = x.astype(jnp.float32)
    rinv = lax.rsqrt(lax.optimization_barrier(jnp.mean(xf * xf, axis=-1, keepdims=True)) + 1e-05)
    hidden = (xf * rinv).astype(jnp.bfloat16).astype(jnp.float32)
    hidden = hidden.reshape(N_DP, MICRO * MB, D)
    deltas = deltas.reshape(MICRO, N_DP, MB, R).transpose(1, 0, 2, 3).reshape(N_DP, MICRO * MB, R)
    partial_value = jnp.einsum('jtd,jtr->jdr', hidden, deltas.astype(jnp.float32)) * scale
    partial_value = lax.optimization_barrier(partial_value.astype(jnp.bfloat16))
    grad = lax.optimization_barrier(jnp.sum(partial_value.astype(jnp.float32), axis=0))
    moment_a = 0.9 * first.astype(jnp.float32) + 0.1 * grad
    moment_b = 0.95 * second.astype(jnp.float32) + 0.05 * grad * grad
    new_master = master - 0.02 * (moment_a / (jnp.sqrt(moment_b) + 1e-08) + 0.1 * master)
    return (new_master, moment_a.astype(jnp.bfloat16), moment_b.astype(jnp.bfloat16))

def reference(section_inputs, grad_first, value_master, first_moment, second_moment, output_weight):
    blocks = section_inputs.reshape(SECTIONS, N_DP, MICRO, MB, D)
    grads = grad_first
    saved = []
    for step in range(MICRO):
        x_step = blocks[:, :, step].reshape(SECTIONS, N_DP * MB, D)
        delta, dx = lax.map(lambda a: section_backward(a[0], a[1], a[2], a[3]), (x_step, grads, value_master, output_weight))
        saved.append(delta)
        grads = jnp.roll(dx, -1, axis=0)
    deltas = jnp.stack(saved, axis=1)
    return lax.map(section_update, (section_inputs, deltas, value_master, first_moment, second_moment))
```

```python
import math

import jax
import jax.numpy as jnp
from jax import lax
from jax.experimental import pallas as pl
from jax.experimental.pallas import tpu as pltpu
from jax.sharding import PartitionSpec as P

MESH = pl.DeviceIdType.MESH
BF16 = jnp.bfloat16
F32 = jnp.float32

D = 4096
R = 512
TOK = 256
ROW = 32
STAGES = TOK // ROW
N_DP = 16
SECTIONS = 32
BLK = D // N_DP
CHUNKS = 4
WIDE = D // CHUNKS
PER = WIDE // BLK
HALF = 8
SCALE = 1.0 / math.sqrt(D)

NT = (((1,), (1,)), ((), ()))
TN = (((0,), (0,)), ((), ()))


def lap_kernel(
    x_hbm, g_hbm, m_hbm, first_hbm, second_hbm, ow_hbm,
    master_out, first_out, second_out,
    x_v, g_v, m_v, first_v, second_v, w_all, o_all, h_v, rinv_v, u_v, f_v, back_v,
    du_all, h_got, acc, z_out, z_in, dx_v,
    local_sem, ag_send, ag_recv, relay_send, relay_recv, h_send, h_recv,
    du_send, du_recv, z_send, z_recv,
):
    s = lax.axis_index("section")
    d = lax.axis_index("dp")
    zh, x, c = d // 8, (d // 2) % 4, d % 2
    me8 = d % 8

    def dp_of(zsel, dx, flip):
        z = zh if zsel == 0 else 1 - zh
        core = c if flip == 0 else 1 - c
        return z * 8 + ((x + dx + 4) % 4) * 2 + core

    def on_dp(zsel, dx, flip):
        return (s, dp_of(zsel, dx, flip))

    behind = ((s + SECTIONS - 1) % SECTIONS, d)
    ahead = ((s + 1) % SECTIONS, d)
    right, left = on_dp(0, 1, 0), on_dp(0, -1, 0)
    sibling, across = on_dp(0, 0, 1), on_dp(1, 0, 0)

    loads = {}

    def load(name, src, dst, at):
        loads[name] = pltpu.make_async_copy(src, dst, local_sem.at[at])
        loads[name].start()

    load("m", m_hbm.at[0], m_v, 0)
    load("ow", ow_hbm.at[0], o_all.at[d], 1)
    load("x", x_hbm.at[0], x_v, 2)
    for t in range(2):
        for n in range(CHUNKS):
            load(
                ("g", t, n),
                g_hbm.at[0, pl.ds(t * ROW, ROW), pl.ds(n * WIDE, WIDE)],
                g_v.at[t, n],
                5 + t * CHUNKS + n,
            )
    load("first", first_hbm.at[0], first_v, 3)
    load("second", second_hbm.at[0], second_v, 4)

    barrier = pltpu.get_barrier_semaphore()
    greet = [behind, ahead, across] + [(s, zh * 8 + (me8 + i) % 8) for i in range(1, 8)]
    for other in greet:
        pl.semaphore_signal(barrier, inc=1, device_id=other, device_id_type=MESH)

    loads["m"].wait()
    w_all[d] = m_v[...].astype(BF16)
    loads["ow"].wait()
    pl.semaphore_wait(barrier, len(greet))

    sends = []

    def piece(p, owner):
        if p < 2:
            return w_all.at[owner, pl.ds(p * (BLK // 2), BLK // 2)]
        return o_all.at[owner, pl.ds((p - 2) * (R // 2), R // 2)]

    def pass_on(p, owner, target):
        copy = pltpu.make_async_remote_copy(
            src_ref=piece(p, owner), dst_ref=piece(p, owner),
            send_sem=ag_send.at[len(sends)], recv_sem=ag_recv.at[p, owner],
            device_id=target, device_id_type=MESH,
        )
        copy.start()
        sends.append(copy)

    def arrived(p, owner):
        pltpu.make_async_remote_copy(
            src_ref=piece(p, owner), dst_ref=piece(p, owner),
            send_sem=ag_send.at[0], recv_sem=ag_recv.at[p, owner],
            device_id=sibling, device_id_type=MESH,
        ).wait_recv()

    for p in range(4):
        for target in (across, right, left, sibling):
            pass_on(p, d, target)

    def handle(p, zsel, dx):
        owner = dp_of(zsel, dx, 0)
        arrived(p, owner)
        if dx == 0 or (dx == -1 and p % 2 == 0):
            pass_on(p, owner, right)
        if dx == 0 or (dx == 1 and p % 2 == 1):
            pass_on(p, owner, left)
        pass_on(p, owner, sibling)

    def from_sibling(pieces, zsel):
        for p in pieces:
            for dx in (0, 1, -1, 2):
                arrived(p, dp_of(zsel, dx, 1))

    loads["x"].wait()

    def normalise(t, carry):
        xs = x_v[pl.ds(pl.multiple_of(t * ROW, ROW), ROW), :].astype(F32)
        rinv = lax.rsqrt(jnp.sum(xs * xs, axis=-1, keepdims=True) * (1.0 / D) + 1e-05)
        rinv_v[t] = rinv
        hidden = (xs * rinv).astype(BF16)
        for j in range(N_DP):
            h_v[j, t] = hidden[:, j * BLK : (j + 1) * BLK]
        return carry

    lax.fori_loop(0, STAGES, normalise, 0)
    u_v[...] = jnp.zeros_like(u_v)
    back_v[...] = jnp.zeros_like(back_v)
    for t in range(2):
        for n in range(CHUNKS):
            loads["g", t, n].wait()

    def upper(zsel):
        base = (zh if zsel == 0 else 1 - zh) * HALF

        def one(i, carry):
            j = base + i
            part = jnp.dot(
                h_v[j].reshape(TOK, BLK), w_all[j], preferred_element_type=F32
            )
            u_v[...] += part.reshape(STAGES, ROW, R)
            return carry

        lax.fori_loop(0, HALF, one, 0)

    def onto(total, grads, n):
        for i in range(PER):
            total = total + lax.dot_general(
                grads[:, i * BLK : (i + 1) * BLK], o_all[n * PER + i], NT,
                preferred_element_type=F32,
            )
        return total

    def first_back(zsel):
        base = (zh if zsel == 0 else 1 - zh) * (HALF // PER)

        def one(i, carry):
            n = base + i
            total = back_v[...].reshape(2 * ROW, R)
            grads = g_v[0:2, n].reshape(2 * ROW, WIDE)
            back_v[...] = onto(total, grads, n).reshape(2, ROW, R)
            return carry

        lax.fori_loop(0, HALF // PER, one, 0)

    for event in (
        (0, 0, -1), (0, 0, 1), (1, 0, -1), (1, 0, 1), (0, 1, 0),
        (2, 0, -1), (2, 0, 1), (3, 0, -1), (3, 0, 1), (0, 0, 2), (1, 1, 0), (1, 0, 2),
    ):
        handle(*event)
    from_sibling((0, 1), 0)
    upper(0)
    for event in (
        (2, 0, 2), (3, 0, 2), (0, 1, -1), (0, 1, 1), (2, 1, 0),
        (1, 1, -1), (1, 1, 1), (0, 1, 2), (1, 1, 2),
    ):
        handle(*event)
    from_sibling((2, 3), 0)
    first_back(0)
    for event in ((3, 1, 0), (2, 1, -1), (2, 1, 1)):
        handle(*event)
    from_sibling((0, 1), 1)
    upper(1)

    def gate(t, carry):
        u = u_v[t] * SCALE
        sig = jax.nn.sigmoid(u)
        u_v[t] = u
        f_v[t] = sig * (1.0 + u * (1.0 - sig))
        return carry

    lax.fori_loop(0, STAGES, gate, 0)
    for event in ((2, 1, 2), (3, 1, -1), (3, 1, 1), (3, 1, 2)):
        handle(*event)
    from_sibling((2, 3), 1)
    first_back(1)

    def relay_copy(t, n):
        return pltpu.make_async_remote_copy(
            src_ref=dx_v.at[t, n], dst_ref=g_v.at[t + 2, n],
            send_sem=relay_send.at[t, n], recv_sem=relay_recv.at[t, n],
            device_id=behind, device_id_type=MESH,
        )

    def du_copy(t, i):
        return pltpu.make_async_remote_copy(
            src_ref=du_all.at[t, me8], dst_ref=du_all.at[t, me8],
            send_sem=du_send.at[t, i], recv_sem=du_recv.at[t, i],
            device_id=(s, zh * 8 + (me8 + i) % 8), device_id_type=MESH,
        )

    def du_arrived(t, i):
        src = (me8 + 8 - i) % 8
        pltpu.make_async_remote_copy(
            src_ref=du_all.at[t, src], dst_ref=du_all.at[t, src],
            send_sem=du_send.at[t, i], recv_sem=du_recv.at[t, i],
            device_id=sibling, device_id_type=MESH,
        ).wait_recv()

    def stage(t, arrives, leaves):
        if arrives:

            def take(n, total):
                relay_copy(t - 2, n).wait_recv()
                return onto(total, g_v[t, n], n)

            back = lax.fori_loop(0, CHUNKS, take, jnp.zeros((ROW, R), F32))
        else:
            back = back_v[t]
        du = (back * f_v[t]).astype(BF16)
        du_all[t, me8] = du
        if leaves:
            rinv = rinv_v[t]
            coef = jnp.sum(du.astype(F32) * u_v[t], axis=-1, keepdims=True) * (1.0 / D)
            coef = coef * rinv * rinv
            gain = rinv * SCALE
            rows = pl.ds(pl.multiple_of(t * ROW, ROW), ROW)

            def give(n, carry):
                wide = w_all[pl.ds(n * PER, PER)].reshape(WIDE, R)
                dh = lax.dot_general(du, wide, NT, preferred_element_type=F32)
                xs = x_v[rows, pl.ds(pl.multiple_of(n * WIDE, WIDE), WIDE)].astype(F32)
                dx = g_v[t, n].astype(F32) + gain * dh - xs * coef
                dx_v[t, n] = dx.astype(BF16)
                relay_copy(t, n).start()
                return carry

            lax.fori_loop(0, CHUNKS, give, 0)
        for i in range(1, 8):
            du_copy(t, i).start()

    def plain(arrives, leaves):
        def one(t, carry):
            stage(t, arrives, leaves)
            return carry

        return one

    lax.fori_loop(0, 2, plain(False, True), 0)

    def h_copy(i, zsel):
        to = (me8 + i) % 8
        block = (zh if zsel == 0 else 1 - zh) * 8 + to
        return pltpu.make_async_remote_copy(
            src_ref=h_v.at[block], dst_ref=h_got.at[zsel, :, me8],
            send_sem=h_send.at[i, zsel], recv_sem=h_recv.at[i, zsel],
            device_id=(s, zh * 8 + to), device_id_type=MESH,
        )

    def h_arrived(i, zsel):
        src = (me8 + 8 - i) % 8
        pltpu.make_async_remote_copy(
            src_ref=h_v.at[0], dst_ref=h_got.at[zsel, :, src],
            send_sem=h_send.at[i, zsel], recv_sem=h_recv.at[i, zsel],
            device_id=sibling, device_id_type=MESH,
        ).wait_recv()

    for i in range(1, 8):
        for zsel in range(2):
            h_copy(i, zsel).start()
    for zsel in range(2):
        h_got[zsel, :, me8] = h_v[dp_of(zsel, 0, 0)]

    lax.fori_loop(2, 6, plain(True, True), 0)
    acc[...] = jnp.zeros_like(acc)

    def gradient(t, carry):
        for i in range(1, 8):
            du_arrived(t, i)
        du = du_all[t].reshape(HALF * ROW, R)
        for zsel in (1, 0):
            acc[zsel] += lax.dot_general(
                h_got[zsel, t].reshape(HALF * ROW, BLK), du, TN,
                preferred_element_type=F32,
            )
        return carry

    for i in range(1, 8):
        for zsel in range(2):
            h_arrived(i, zsel)
    lax.fori_loop(0, 4, gradient, 0)
    stage(6, True, False)
    lax.fori_loop(4, 6, gradient, 0)
    stage(7, True, False)
    lax.fori_loop(6, 8, gradient, 0)

    def z_copy(i):
        part = pl.ds(i * (BLK // 2), BLK // 2)
        return pltpu.make_async_remote_copy(
            src_ref=z_out.at[part], dst_ref=z_in.at[part],
            send_sem=z_send.at[i], recv_sem=z_recv.at[i],
            device_id=across, device_id_type=MESH,
        )

    for i in range(2):
        part = pl.ds(i * (BLK // 2), BLK // 2)
        z_out[part] = (acc[1, part] * SCALE).astype(BF16)
        z_copy(i).start()
    loads["first"].wait()
    loads["second"].wait()
    for i in range(2):
        part = pl.ds(i * (BLK // 2), BLK // 2)
        z_copy(i).wait_recv()
        grad = acc[0, part] * SCALE + z_in[part].astype(F32)
        moment_a = 0.9 * first_v[part].astype(F32) + 0.1 * grad
        moment_b = 0.95 * second_v[part].astype(F32) + 0.05 * grad * grad
        master = m_v[part]
        master_out[part] = master - 0.02 * (
            moment_a / (jnp.sqrt(moment_b) + 1e-08) + 0.1 * master
        )
        first_out[part] = moment_a.astype(BF16)
        second_out[part] = moment_b.astype(BF16)

    for copy in sends:
        copy.wait_send()

    def sent(t, carry):
        for i in range(1, 8):
            du_copy(t, i).wait_send()
        return carry

    def relayed(t, carry):
        for n in range(CHUNKS):
            relay_copy(t, n).wait_send()
        return carry

    lax.fori_loop(0, STAGES, sent, 0)
    lax.fori_loop(0, 6, relayed, 0)
    for i in range(1, 8):
        for zsel in range(2):
            h_copy(i, zsel).wait_send()
    for i in range(2):
        z_copy(i).wait_send()


def on_device(section_inputs, grad_first, value_master, first_moment, second_moment, output_weight):
    dma = pltpu.SemaphoreType.DMA
    outs = pl.pallas_call(
        lap_kernel,
        name="lap",
        out_shape=(
            jax.ShapeDtypeStruct((BLK, R), F32),
            jax.ShapeDtypeStruct((BLK, R), BF16),
            jax.ShapeDtypeStruct((BLK, R), BF16),
        ),
        in_specs=[pl.BlockSpec(memory_space=pl.ANY)] * 6,
        out_specs=[pl.BlockSpec(memory_space=pltpu.VMEM)] * 3,
        scratch_shapes=[
            pltpu.VMEM((TOK, D), BF16),
            pltpu.VMEM((STAGES, CHUNKS, ROW, WIDE), BF16),
            pltpu.VMEM((BLK, R), F32),
            pltpu.VMEM((BLK, R), BF16),
            pltpu.VMEM((BLK, R), BF16),
            pltpu.VMEM((N_DP, BLK, R), BF16),
            pltpu.VMEM((N_DP, R, BLK), BF16),
            pltpu.VMEM((N_DP, STAGES, ROW, BLK), BF16),
            pltpu.VMEM((STAGES, ROW, 1), F32),
            pltpu.VMEM((STAGES, ROW, R), F32),
            pltpu.VMEM((STAGES, ROW, R), F32),
            pltpu.VMEM((2, ROW, R), F32),
            pltpu.VMEM((STAGES, HALF, ROW, R), BF16),
            pltpu.VMEM((2, STAGES, HALF, ROW, BLK), BF16),
            pltpu.VMEM((2, BLK, R), F32),
            pltpu.VMEM((BLK, R), BF16),
            pltpu.VMEM((BLK, R), BF16),
            pltpu.VMEM((6, CHUNKS, ROW, WIDE), BF16),
            dma((5 + 2 * CHUNKS,)),
            dma((64,)),
            dma((4, N_DP)),
            dma((6, CHUNKS)),
            dma((6, CHUNKS)),
            dma((8, 2)),
            dma((8, 2)),
            dma((STAGES, 8)),
            dma((STAGES, 8)),
            dma((2,)),
            dma((2,)),
        ],
        compiler_params=pltpu.CompilerParams(
            collective_id=0, has_side_effects=True, vmem_limit_bytes=48 * 1024 * 1024
        ),
        cost_estimate=pl.CostEstimate(flops=4 * 10**9, bytes_accessed=5 * 2**20, transcendentals=0),
    )(section_inputs, grad_first, value_master, first_moment, second_moment, output_weight)
    return tuple(out[None] for out in outs)


def solution(mesh):
    rows = P("section", "dp", None)
    return jax.shard_map(
        on_device,
        mesh=mesh,
        in_specs=(rows, rows, rows, rows, rows, P("section", None, "dp")),
        out_specs=(rows, rows, rows),
        check_vma=False,
    )
```

```python
import math

import jax
import jax.numpy as jnp
from jax import lax
from jax.experimental import pallas as pl
from jax.experimental.pallas import tpu as pltpu
from jax.sharding import PartitionSpec as P

MESH = pl.DeviceIdType.MESH
BF16 = jnp.bfloat16
F32 = jnp.float32

D = 4096
R = 512
TOK = 256
ROW = 32
STAGES = TOK // ROW
N_DP = 16
SECTIONS = 32
BLK = D // N_DP
CHUNKS = 4
WIDE = D // CHUNKS
PER = WIDE // BLK
HALF = 8
EARLY = 6
LATE = STAGES - EARLY
SCALE = 1.0 / math.sqrt(D)

NT = (((1,), (1,)), ((), ()))
TN = (((0,), (0,)), ((), ()))


def lap_kernel(
    x_hbm, g_hbm, m_hbm, ow_hbm, grad_out,
    x_v, g_v, m_v, w_all, o_all, h_v, rinv_v, u_v, f_v, back_v,
    du_all, du_far, h_got, h_cross, h_far, acc, z_out, z_in, dx_v,
    local_sem, ag_send, ag_recv, relay_send, relay_recv, h_send, h_recv,
    du_send, du_recv, cross_send, cross_recv, far_send, far_recv, hf_send, hf_recv,
    z_send, z_recv,
):
    s = lax.axis_index("section")
    d = lax.axis_index("dp")
    zh, x, c = d // 8, (d // 2) % 4, d % 2
    me8 = d % 8

    def dp_of(zsel, dx, flip):
        z = zh if zsel == 0 else 1 - zh
        core = c if flip == 0 else 1 - c
        return z * 8 + ((x + dx + 4) % 4) * 2 + core

    def on_dp(zsel, dx, flip):
        return (s, dp_of(zsel, dx, flip))

    behind = ((s + SECTIONS - 1) % SECTIONS, d)
    ahead = ((s + 1) % SECTIONS, d)
    right, left = on_dp(0, 1, 0), on_dp(0, -1, 0)
    sibling, across = on_dp(0, 0, 1), on_dp(1, 0, 0)

    loads = {}

    def load(name, src, dst, at):
        loads[name] = pltpu.make_async_copy(src, dst, local_sem.at[at])
        loads[name].start()

    load("m", m_hbm.at[0], m_v, 0)
    load("ow", ow_hbm.at[0], o_all.at[d], 1)
    load("x", x_hbm.at[0], x_v, 2)
    for t in range(2):
        for n in range(CHUNKS):
            load(
                ("g", t, n),
                g_hbm.at[0, pl.ds(t * ROW, ROW), pl.ds(n * WIDE, WIDE)],
                g_v.at[t, n],
                3 + t * CHUNKS + n,
            )

    barrier = pltpu.get_barrier_semaphore()
    greet = [behind, ahead, across] + [(s, zh * 8 + (me8 + i) % 8) for i in range(1, 8)]
    for other in greet:
        pl.semaphore_signal(barrier, inc=1, device_id=other, device_id_type=MESH)

    loads["m"].wait()
    w_all[d] = m_v[...].astype(BF16)
    loads["ow"].wait()
    pl.semaphore_wait(barrier, len(greet))

    sends = []

    def piece(p, owner):
        if p < 2:
            return w_all.at[owner, pl.ds(p * (BLK // 2), BLK // 2)]
        return o_all.at[owner, pl.ds((p - 2) * (R // 2), R // 2)]

    def pass_on(p, owner, target):
        copy = pltpu.make_async_remote_copy(
            src_ref=piece(p, owner), dst_ref=piece(p, owner),
            send_sem=ag_send.at[len(sends)], recv_sem=ag_recv.at[p, owner],
            device_id=target, device_id_type=MESH,
        )
        copy.start()
        sends.append(copy)

    def arrived(p, owner):
        pltpu.make_async_remote_copy(
            src_ref=piece(p, owner), dst_ref=piece(p, owner),
            send_sem=ag_send.at[0], recv_sem=ag_recv.at[p, owner],
            device_id=sibling, device_id_type=MESH,
        ).wait_recv()

    for p in range(4):
        for target in (across, right, left, sibling):
            pass_on(p, d, target)

    def handle(p, zsel, dx):
        owner = dp_of(zsel, dx, 0)
        arrived(p, owner)
        if dx == 0 or (dx == -1 and p % 2 == 0):
            pass_on(p, owner, right)
        if dx == 0 or (dx == 1 and p % 2 == 1):
            pass_on(p, owner, left)
        pass_on(p, owner, sibling)

    def from_sibling(pieces, zsel):
        for p in pieces:
            for dx in (0, 1, -1, 2):
                arrived(p, dp_of(zsel, dx, 1))

    loads["x"].wait()

    def normalise(t, carry):
        xs = x_v[pl.ds(pl.multiple_of(t * ROW, ROW), ROW), :].astype(F32)
        rinv = lax.rsqrt(jnp.sum(xs * xs, axis=-1, keepdims=True) * (1.0 / D) + 1e-05)
        rinv_v[t] = rinv
        hidden = (xs * rinv).astype(BF16)
        for j in range(N_DP):
            h_v[j, t] = hidden[:, j * BLK : (j + 1) * BLK]
        return carry

    lax.fori_loop(0, STAGES, normalise, 0)
    u_v[...] = jnp.zeros_like(u_v)
    back_v[...] = jnp.zeros_like(back_v)
    for t in range(2):
        for n in range(CHUNKS):
            loads["g", t, n].wait()

    def upper(zsel):
        base = (zh if zsel == 0 else 1 - zh) * HALF

        def one(i, carry):
            j = base + i
            part = jnp.dot(
                h_v[j].reshape(TOK, BLK), w_all[j], preferred_element_type=F32
            )
            u_v[...] += part.reshape(STAGES, ROW, R)
            return carry

        lax.fori_loop(0, HALF, one, 0)

    def onto(total, grads, n):
        for i in range(PER):
            total = total + lax.dot_general(
                grads[:, i * BLK : (i + 1) * BLK], o_all[n * PER + i], NT,
                preferred_element_type=F32,
            )
        return total

    def first_back(zsel):
        base = (zh if zsel == 0 else 1 - zh) * (HALF // PER)

        def one(i, carry):
            n = base + i
            total = back_v[...].reshape(2 * ROW, R)
            grads = g_v[0:2, n].reshape(2 * ROW, WIDE)
            back_v[...] = onto(total, grads, n).reshape(2, ROW, R)
            return carry

        lax.fori_loop(0, HALF // PER, one, 0)

    hidden_across = pltpu.make_async_remote_copy(
        src_ref=h_v.at[pl.ds((1 - zh) * HALF, HALF), pl.ds(EARLY, LATE)], dst_ref=h_cross,
        send_sem=hf_send.at[0], recv_sem=hf_recv.at[0],
        device_id=across, device_id_type=MESH,
    )

    for event in (
        (0, 0, -1), (0, 0, 1), (1, 0, -1), (1, 0, 1), (0, 1, 0),
        (2, 0, -1), (2, 0, 1), (3, 0, -1), (3, 0, 1), (0, 0, 2), (1, 1, 0), (1, 0, 2),
    ):
        handle(*event)
    from_sibling((0, 1), 0)
    upper(0)
    for event in (
        (2, 0, 2), (3, 0, 2), (0, 1, -1), (0, 1, 1), (2, 1, 0),
        (1, 1, -1), (1, 1, 1), (0, 1, 2), (1, 1, 2),
    ):
        handle(*event)
    from_sibling((2, 3), 0)
    first_back(0)
    handle(3, 1, 0)
    hidden_across.start()
    for event in ((2, 1, -1), (2, 1, 1)):
        handle(*event)
    from_sibling((0, 1), 1)
    upper(1)

    def gate(t, carry):
        u = u_v[t] * SCALE
        sig = jax.nn.sigmoid(u)
        u_v[t] = u
        f_v[t] = sig * (1.0 + u * (1.0 - sig))
        return carry

    lax.fori_loop(0, STAGES, gate, 0)
    for event in ((2, 1, 2), (3, 1, -1), (3, 1, 1), (3, 1, 2)):
        handle(*event)
    from_sibling((2, 3), 1)
    first_back(1)

    def relay_copy(t, n):
        return pltpu.make_async_remote_copy(
            src_ref=dx_v.at[t, n], dst_ref=g_v.at[t + 2, n],
            send_sem=relay_send.at[t, n], recv_sem=relay_recv.at[t, n],
            device_id=behind, device_id_type=MESH,
        )

    def mate(i):
        return (s, zh * 8 + (me8 + i) % 8)

    sib8 = 2 * x + 1 - c

    def du_copy(t, src, i, target):
        return pltpu.make_async_remote_copy(
            src_ref=du_all.at[t, src], dst_ref=du_all.at[t, src],
            send_sem=du_send.at[t, i], recv_sem=du_recv.at[t, src],
            device_id=target, device_id_type=MESH,
        )

    def rail(t):
        return [du_copy(t, me8, i, mate(2 * i)) for i in (1, 3, 2)] + [
            du_copy(t, me8, 0, sibling)
        ]

    def spread(t):
        return [du_copy(t, me8, i, mate(i)) for i in range(1, 8)]

    def passed(t):
        return [du_copy(t, (me8 + 2 * i) % 8, 3 + i, sibling) for i in (1, 3, 2)]

    def pass_rail(t):
        for copy in passed(t):
            copy.wait_recv()
            copy.start()

    def cross_copy(k):
        return pltpu.make_async_remote_copy(
            src_ref=du_all.at[EARLY + k, me8], dst_ref=du_far.at[k, me8],
            send_sem=cross_send.at[k], recv_sem=cross_recv.at[k],
            device_id=across, device_id_type=MESH,
        )

    def far_copy(k, i, src):
        return pltpu.make_async_remote_copy(
            src_ref=du_far.at[k, src], dst_ref=du_far.at[k, src],
            send_sem=far_send.at[k, i], recv_sem=far_recv.at[k, src],
            device_id=mate(i), device_id_type=MESH,
        )

    def spread_far(k):
        cross_copy(k).wait_recv()
        for i in range(1, 8):
            far_copy(k, i, me8).start()

    def stage(t, arrives, leaves):
        if arrives:

            def take(n, total):
                relay_copy(t - 2, n).wait_recv()
                return onto(total, g_v[t, n], n)

            back = lax.fori_loop(0, CHUNKS, take, jnp.zeros((ROW, R), F32))
        else:
            back = back_v[t]
        du = (back * f_v[t]).astype(BF16)
        du_all[t, me8] = du
        if leaves:
            rinv = rinv_v[t]
            coef = jnp.sum(du.astype(F32) * u_v[t], axis=-1, keepdims=True) * (1.0 / D)
            coef = coef * rinv * rinv
            gain = rinv * SCALE
            rows = pl.ds(pl.multiple_of(t * ROW, ROW), ROW)

            def give(n, carry):
                wide = w_all[pl.ds(n * PER, PER)].reshape(WIDE, R)
                dh = lax.dot_general(du, wide, NT, preferred_element_type=F32)
                xs = x_v[rows, pl.ds(pl.multiple_of(n * WIDE, WIDE), WIDE)].astype(F32)
                dx = g_v[t, n].astype(F32) + gain * dh - xs * coef
                dx_v[t, n] = dx.astype(BF16)
                relay_copy(t, n).start()
                return carry

            lax.fori_loop(0, CHUNKS, give, 0)
        return du

    def plain(arrives, leaves):
        def one(t, carry):
            stage(t, arrives, leaves)
            for copy in rail(t):
                copy.start()
            return carry

        return one

    def h_copy(i, zsel, src):
        to = (me8 + i) % 8
        block = (zh if zsel == 0 else 1 - zh) * 8 + to
        count = STAGES if zsel == 0 else EARLY
        return pltpu.make_async_remote_copy(
            src_ref=h_v.at[block, pl.ds(0, count)], dst_ref=h_got.at[zsel, pl.ds(0, count), src],
            send_sem=h_send.at[i, zsel], recv_sem=h_recv.at[i, zsel],
            device_id=mate(i), device_id_type=MESH,
        )

    def hf_copy(i, src):
        return pltpu.make_async_remote_copy(
            src_ref=h_cross.at[(me8 + i) % 8], dst_ref=h_far.at[:, src],
            send_sem=hf_send.at[i], recv_sem=hf_recv.at[i],
            device_id=mate(i), device_id_type=MESH,
        )

    def begin_hidden():
        for i in (2, 6, 4, 3, 7, 5, 1):
            for zsel in (1, 0):
                h_copy(i, zsel, me8).start()
        for zsel in range(2):
            h_got[zsel, :, me8] = h_v[dp_of(zsel, 0, 0)]
        acc[...] = jnp.zeros_like(acc)

    def spread_hidden():
        hidden_across.wait_recv()
        for i in range(1, 8):
            hf_copy(i, me8).start()
        h_far[:, me8] = h_cross[me8]

    def gradient(t, carry):
        for i in range(4):
            du_copy(t, 2 * i + 1 - c, 0, sibling).wait_recv()
        du = du_all[t].reshape(HALF * ROW, R)
        for zsel in (1, 0):
            acc[zsel] += lax.dot_general(
                h_got[zsel, t].reshape(HALF * ROW, BLK), du, TN,
                preferred_element_type=F32,
            )
        return carry

    def late_gradient(k):
        for i in range(1, 8):
            du_copy(EARLY + k, (me8 + i) % 8, 0, sibling).wait_recv()
        acc[0] += lax.dot_general(
            h_got[0, EARLY + k].reshape(HALF * ROW, BLK),
            du_all[EARLY + k].reshape(HALF * ROW, R), TN, preferred_element_type=F32,
        )

    def far_gradient(k):
        for i in range(1, 8):
            far_copy(k, i, (me8 + i) % 8).wait_recv()
        acc[0] += lax.dot_general(
            h_far[k].reshape(HALF * ROW, BLK),
            du_far[k].reshape(HALF * ROW, R), TN, preferred_element_type=F32,
        )

    def z_copy(i):
        part = pl.ds(i * (BLK // 2), BLK // 2)
        return pltpu.make_async_remote_copy(
            src_ref=z_out.at[part], dst_ref=z_in.at[part],
            send_sem=z_send.at[i], recv_sem=z_recv.at[i],
            device_id=across, device_id_type=MESH,
        )

    lax.fori_loop(0, 2, plain(False, True), 0)
    begin_hidden()
    lax.fori_loop(2, 5, plain(True, True), 0)
    spread_hidden()
    pass_rail(0)
    pass_rail(1)
    lax.fori_loop(5, 6, plain(True, True), 0)
    pass_rail(2)
    pass_rail(3)
    for i in range(1, 8):
        for zsel in range(2):
            h_copy(i, zsel, (me8 + 8 - i) % 8).wait_recv()
    lax.fori_loop(0, 3, gradient, 0)
    pass_rail(4)

    def finish_early():
        pass_rail(5)
        lax.fori_loop(3, EARLY, gradient, 0)
        for i in range(2):
            part = pl.ds(i * (BLK // 2), BLK // 2)
            z_out[part] = (acc[1, part] * SCALE).astype(BF16)
            z_copy(i).start()

    for k in range(LATE):
        stage(EARLY + k, True, False)
        cross_copy(k).start()
        for copy in spread(EARLY + k):
            copy.start()
        if k == 0:
            finish_early()
            spread_far(k)
            for i in range(1, 8):
                hf_copy(i, (me8 + 8 - i) % 8).wait_recv()
            late_gradient(k)
            far_gradient(k)
    spread_far(LATE - 1)
    late_gradient(LATE - 1)
    far_gradient(LATE - 1)

    for i in range(2):
        part = pl.ds(i * (BLK // 2), BLK // 2)
        z_copy(i).wait_recv()
        grad_out[part] = acc[0, part] * SCALE + z_in[part].astype(F32)

    for copy in sends:
        copy.wait_send()

    def sent(t, carry):
        for copy in rail(t) + passed(t):
            copy.wait_send()
        return carry

    def relayed(t, carry):
        for n in range(CHUNKS):
            relay_copy(t, n).wait_send()
        return carry

    lax.fori_loop(0, EARLY, sent, 0)
    lax.fori_loop(0, EARLY, relayed, 0)
    hidden_across.wait_send()
    for i in range(1, 8):
        hf_copy(i, me8).wait_send()
        for zsel in range(2):
            h_copy(i, zsel, me8).wait_send()
    for k in range(LATE):
        cross_copy(k).wait_send()
        for copy in spread(EARLY + k):
            copy.wait_send()
        for i in range(1, 8):
            far_copy(k, i, me8).wait_send()
    for i in range(2):
        z_copy(i).wait_send()


def on_device(section_inputs, grad_first, value_master, first_moment, second_moment, output_weight):
    dma = pltpu.SemaphoreType.DMA
    grad = pl.pallas_call(
        lap_kernel,
        name="lap",
        out_shape=jax.ShapeDtypeStruct((BLK, R), F32),
        in_specs=[pl.BlockSpec(memory_space=pl.ANY)] * 4,
        out_specs=pl.BlockSpec(memory_space=pltpu.VMEM),
        scratch_shapes=[
            pltpu.VMEM((TOK, D), BF16),
            pltpu.VMEM((STAGES, CHUNKS, ROW, WIDE), BF16),
            pltpu.VMEM((BLK, R), F32),
            pltpu.VMEM((N_DP, BLK, R), BF16),
            pltpu.VMEM((N_DP, R, BLK), BF16),
            pltpu.VMEM((N_DP, STAGES, ROW, BLK), BF16),
            pltpu.VMEM((STAGES, ROW, 1), F32),
            pltpu.VMEM((STAGES, ROW, R), F32),
            pltpu.VMEM((STAGES, ROW, R), F32),
            pltpu.VMEM((2, ROW, R), F32),
            pltpu.VMEM((STAGES, HALF, ROW, R), BF16),
            pltpu.VMEM((LATE, HALF, ROW, R), BF16),
            pltpu.VMEM((2, STAGES, HALF, ROW, BLK), BF16),
            pltpu.VMEM((HALF, LATE, ROW, BLK), BF16),
            pltpu.VMEM((LATE, HALF, ROW, BLK), BF16),
            pltpu.VMEM((2, BLK, R), F32),
            pltpu.VMEM((BLK, R), BF16),
            pltpu.VMEM((BLK, R), BF16),
            pltpu.VMEM((6, CHUNKS, ROW, WIDE), BF16),
            dma((3 + 2 * CHUNKS,)),
            dma((64,)),
            dma((4, N_DP)),
            dma((6, CHUNKS)),
            dma((6, CHUNKS)),
            dma((8, 2)),
            dma((8, 2)),
            dma((STAGES, 8)),
            dma((STAGES, 8)),
            dma((LATE,)),
            dma((LATE,)),
            dma((LATE, 8)),
            dma((LATE, 8)),
            dma((8,)),
            dma((8,)),
            dma((2,)),
            dma((2,)),
        ],
        compiler_params=pltpu.CompilerParams(
            collective_id=0, has_side_effects=True, vmem_limit_bytes=60 * 1024 * 1024
        ),
        cost_estimate=pl.CostEstimate(flops=4 * 10**9, bytes_accessed=5 * 2**20, transcendentals=0),
    )(section_inputs, grad_first, value_master, output_weight)
    grad = grad[None]
    moment_a = 0.9 * first_moment.astype(F32) + 0.1 * grad
    moment_b = 0.95 * second_moment.astype(F32) + 0.05 * grad * grad
    master = value_master - 0.02 * (
        moment_a / (jnp.sqrt(moment_b) + 1e-08) + 0.1 * value_master
    )
    return master, moment_a.astype(BF16), moment_b.astype(BF16)


def solution(mesh):
    rows = P("section", "dp", None)
    return jax.shard_map(
        on_device,
        mesh=mesh,
        in_specs=(rows, rows, rows, rows, rows, P("section", None, "dp")),
        out_specs=(rows, rows, rows),
        check_vma=False,
    )
```

```python
import math

import jax
import jax.numpy as jnp
from jax import lax
from jax.experimental import pallas as pl
from jax.experimental.pallas import tpu as pltpu
from jax.sharding import PartitionSpec as P

MESH = pl.DeviceIdType.MESH
BF16 = jnp.bfloat16
F32 = jnp.float32

D = 4096
R = 512
TOK = 256
ROW = 32
STAGES = TOK // ROW
N_DP = 16
SECTIONS = 32
BLK = D // N_DP
CHUNKS = 4
WIDE = D // CHUNKS
PER = WIDE // BLK
HALF = 8
EARLY = 6
LATE = STAGES - EARLY
BEFORE = 1
PARTS = 4
SCALE = 1.0 / math.sqrt(D)

NT = (((1,), (1,)), ((), ()))
TN = (((0,), (0,)), ((), ()))


def lap_kernel(
    x_hbm, g_hbm, m_hbm, ow_hbm, grad_out,
    x_v, g_v, m_v, w_all, o_all, h_v, rinv_v, u_v, f_v, back_v,
    du_all, du_far, h_got, h_cross, h_far, acc, z_out, z_in, dx_v,
    local_sem, ag_send, ag_recv, relay_send, relay_recv, h_send, h_recv,
    du_send, du_recv, cross_send, cross_recv, far_send, far_recv, hf_send, hf_recv,
    z_send, z_recv,
):
    s = lax.axis_index("section")
    d = lax.axis_index("dp")
    zh, x, c = d // 8, (d // 2) % 4, d % 2
    me8 = d % 8

    def dp_of(zsel, dx, flip):
        z = zh if zsel == 0 else 1 - zh
        core = c if flip == 0 else 1 - c
        return z * 8 + ((x + dx + 4) % 4) * 2 + core

    def on_dp(zsel, dx, flip):
        return (s, dp_of(zsel, dx, flip))

    behind = ((s + SECTIONS - 1) % SECTIONS, d)
    ahead = ((s + 1) % SECTIONS, d)
    right, left = on_dp(0, 1, 0), on_dp(0, -1, 0)
    sibling, across = on_dp(0, 0, 1), on_dp(1, 0, 0)

    loads = {}

    def load(name, src, dst, at):
        loads[name] = pltpu.make_async_copy(src, dst, local_sem.at[at])
        loads[name].start()

    load("m", m_hbm.at[0], m_v, 0)
    load("ow", ow_hbm.at[0], o_all.at[d], 1)
    load("x", x_hbm.at[0], x_v, 2)
    for t in range(2):
        for n in range(CHUNKS):
            load(
                ("g", t, n),
                g_hbm.at[0, pl.ds(t * ROW, ROW), pl.ds(n * WIDE, WIDE)],
                g_v.at[t, n],
                3 + t * CHUNKS + n,
            )

    barrier = pltpu.get_barrier_semaphore()
    greet = [behind, ahead, across] + [(s, zh * 8 + (me8 + i) % 8) for i in range(1, 8)]
    for other in greet:
        pl.semaphore_signal(barrier, inc=1, device_id=other, device_id_type=MESH)

    loads["m"].wait()
    w_all[d] = m_v[...].astype(BF16)
    loads["ow"].wait()
    pl.semaphore_wait(barrier, len(greet))

    sends = []

    def piece(p, owner):
        if p < 2:
            return w_all.at[owner, pl.ds(p * (BLK // 2), BLK // 2)]
        return o_all.at[owner, pl.ds((p - 2) * (R // 2), R // 2)]

    def pass_on(p, owner, target):
        copy = pltpu.make_async_remote_copy(
            src_ref=piece(p, owner), dst_ref=piece(p, owner),
            send_sem=ag_send.at[len(sends)], recv_sem=ag_recv.at[p, owner],
            device_id=target, device_id_type=MESH,
        )
        copy.start()
        sends.append(copy)

    def arrived(p, owner):
        pltpu.make_async_remote_copy(
            src_ref=piece(p, owner), dst_ref=piece(p, owner),
            send_sem=ag_send.at[0], recv_sem=ag_recv.at[p, owner],
            device_id=sibling, device_id_type=MESH,
        ).wait_recv()

    for p in range(4):
        for target in ((across,) if p < 2 else ()) + (right, left, sibling):
            pass_on(p, d, target)

    def handle(p, zsel, dx):
        owner = dp_of(zsel, dx, 0)
        arrived(p, owner)
        if dx == 0 or (dx == -1 and p % 2 == 0):
            pass_on(p, owner, right)
        if dx == 0 or (dx == 1 and p % 2 == 1):
            pass_on(p, owner, left)
        pass_on(p, owner, sibling)

    def from_sibling(pieces, zsel):
        for p in pieces:
            for dx in (0, 1, -1, 2):
                arrived(p, dp_of(zsel, dx, 1))

    loads["x"].wait()

    def normalise(t, carry):
        xs = x_v[pl.ds(pl.multiple_of(t * ROW, ROW), ROW), :].astype(F32)
        rinv = lax.rsqrt(jnp.sum(xs * xs, axis=-1, keepdims=True) * (1.0 / D) + 1e-05)
        rinv_v[t] = rinv
        hidden = (xs * rinv).astype(BF16)
        for j in range(N_DP):
            h_v[j, t] = hidden[:, j * BLK : (j + 1) * BLK]
        return carry

    lax.fori_loop(0, STAGES, normalise, 0)
    u_v[...] = jnp.zeros_like(u_v)
    back_v[...] = jnp.zeros_like(back_v)
    for t in range(2):
        for n in range(CHUNKS):
            loads["g", t, n].wait()

    def upper(zsel, first=0, count=HALF):
        base = (zh if zsel == 0 else 1 - zh) * HALF

        def one(i, carry):
            j = base + i
            part = jnp.dot(
                h_v[j].reshape(TOK, BLK), w_all[j], preferred_element_type=F32
            )
            u_v[...] += part.reshape(STAGES, ROW, R)
            return carry

        lax.fori_loop(first, first + count, one, 0)

    def onto(total, grads, n):
        for i in range(PER):
            total = total + lax.dot_general(
                grads[:, i * BLK : (i + 1) * BLK], o_all[n * PER + i], NT,
                preferred_element_type=F32,
            )
        return total

    def first_back(zsel):
        base = (zh if zsel == 0 else 1 - zh) * (HALF // PER)

        def one(i, carry):
            n = base + i
            total = back_v[...].reshape(2 * ROW, R)
            grads = g_v[0:2, n].reshape(2 * ROW, WIDE)
            back_v[...] = onto(total, grads, n).reshape(2, ROW, R)
            return carry

        lax.fori_loop(0, HALF // PER, one, 0)

    hidden_across = pltpu.make_async_remote_copy(
        src_ref=h_v.at[pl.ds((1 - zh) * HALF, HALF), pl.ds(EARLY, LATE)], dst_ref=h_cross,
        send_sem=hf_send.at[0], recv_sem=hf_recv.at[0],
        device_id=across, device_id_type=MESH,
    )

    for event in (
        (0, 0, -1), (0, 0, 1), (1, 0, -1), (1, 0, 1), (0, 1, 0),
        (2, 0, -1), (2, 0, 1), (3, 0, -1), (3, 0, 1), (0, 0, 2), (1, 1, 0), (1, 0, 2),
    ):
        handle(*event)
        if event == (2, 0, -1):
            pass_on(2, d, across)
        if event == (1, 1, 0):
            pass_on(3, d, across)
    from_sibling((0, 1), 0)
    upper(0)
    for event in (
        (2, 0, 2), (3, 0, 2), (0, 1, -1), (0, 1, 1), (2, 1, 0),
        (1, 1, -1), (1, 1, 1), (0, 1, 2), (1, 1, 2),
    ):
        handle(*event)
    from_sibling((2, 3), 0)
    first_back(0)
    handle(3, 1, 0)
    hidden_across.start()
    for event in ((2, 1, -1), (2, 1, 1)):
        handle(*event)
    def gate(t, carry):
        u = u_v[t] * SCALE
        sig = jax.nn.sigmoid(u)
        u_v[t] = u
        f_v[t] = sig * (1.0 + u * (1.0 - sig))
        return carry

    from_sibling((0, 1), 1)
    for i, event in enumerate(((3, 1, -1), (3, 1, 1), (2, 1, 2), (3, 1, 2))):
        handle(*event)
        upper(1, 2 * i, 2)
    lax.fori_loop(0, STAGES, gate, 0)
    from_sibling((2, 3), 1)
    first_back(1)

    def relay_copy(t, n):
        return pltpu.make_async_remote_copy(
            src_ref=dx_v.at[t, n], dst_ref=g_v.at[t + 2, n],
            send_sem=relay_send.at[t, n], recv_sem=relay_recv.at[t, n],
            device_id=behind, device_id_type=MESH,
        )

    def mate(i):
        return (s, zh * 8 + (me8 + i) % 8)

    sib8 = 2 * x + 1 - c

    def du_copy(t, src, i, target):
        return pltpu.make_async_remote_copy(
            src_ref=du_all.at[t, src], dst_ref=du_all.at[t, src],
            send_sem=du_send.at[t, i], recv_sem=du_recv.at[t, src],
            device_id=target, device_id_type=MESH,
        )

    def rail(t):
        return [du_copy(t, me8, i, mate(2 * i)) for i in (1, 3, 2)] + [
            du_copy(t, me8, 0, sibling)
        ]

    def passed(t):
        return [du_copy(t, (me8 + 2 * i) % 8, 3 + i, sibling) for i in (1, 3, 2)]

    def pass_rail(t):
        for copy in passed(t):
            copy.wait_recv()
            copy.start()

    def cross_copy(k):
        return pltpu.make_async_remote_copy(
            src_ref=du_all.at[EARLY + k, me8], dst_ref=du_far.at[k, me8],
            send_sem=cross_send.at[k], recv_sem=cross_recv.at[k],
            device_id=across, device_id_type=MESH,
        )

    def far_copy(k, src, i, target):
        return pltpu.make_async_remote_copy(
            src_ref=du_far.at[k, src], dst_ref=du_far.at[k, src],
            send_sem=far_send.at[k, i], recv_sem=far_recv.at[k, src],
            device_id=target, device_id_type=MESH,
        )

    def far_rail(k):
        return [far_copy(k, me8, i, mate(2 * i)) for i in (1, 3, 2)] + [
            far_copy(k, me8, 0, sibling)
        ]

    def far_passed(k):
        return [far_copy(k, (me8 + 2 * i) % 8, 3 + i, sibling) for i in (1, 3, 2)]

    def begin_far(k):
        cross_copy(k).wait_recv()
        for copy in far_rail(k):
            copy.start()

    def pass_far(k):
        for copy in far_passed(k):
            copy.wait_recv()
            copy.start()

    def stage(t, arrives, leaves):
        if arrives:

            def take(n, total):
                relay_copy(t - 2, n).wait_recv()
                return onto(total, g_v[t, n], n)

            back = lax.fori_loop(0, CHUNKS, take, jnp.zeros((ROW, R), F32))
        else:
            back = back_v[t]
        du = (back * f_v[t]).astype(BF16)
        du_all[t, me8] = du
        if leaves:
            rinv = rinv_v[t]
            coef = jnp.sum(du.astype(F32) * u_v[t], axis=-1, keepdims=True) * (1.0 / D)
            coef = coef * rinv * rinv
            gain = rinv * SCALE
            rows = pl.ds(pl.multiple_of(t * ROW, ROW), ROW)

            def give(n, carry):
                wide = w_all[pl.ds(n * PER, PER)].reshape(WIDE, R)
                dh = lax.dot_general(du, wide, NT, preferred_element_type=F32)
                xs = x_v[rows, pl.ds(pl.multiple_of(n * WIDE, WIDE), WIDE)].astype(F32)
                dx = g_v[t, n].astype(F32) + gain * dh - xs * coef
                dx_v[t, n] = dx.astype(BF16)
                relay_copy(t, n).start()
                return carry

            lax.fori_loop(0, CHUNKS, give, 0)
        return du

    def plain(arrives, leaves):
        def one(t, carry):
            stage(t, arrives, leaves)
            for copy in rail(t):
                copy.start()
            return carry

        return one

    def h_copy(i, zsel, src):
        to = (me8 + i) % 8
        block = (zh if zsel == 0 else 1 - zh) * 8 + to
        count = STAGES if zsel == 0 else EARLY
        return pltpu.make_async_remote_copy(
            src_ref=h_v.at[block, pl.ds(0, count)], dst_ref=h_got.at[zsel, pl.ds(0, count), src],
            send_sem=h_send.at[i, zsel], recv_sem=h_recv.at[i, zsel],
            device_id=mate(i), device_id_type=MESH,
        )

    def hf_copy(i, src):
        return pltpu.make_async_remote_copy(
            src_ref=h_cross.at[(me8 + i) % 8], dst_ref=h_far.at[:, src],
            send_sem=hf_send.at[i], recv_sem=hf_recv.at[i],
            device_id=mate(i), device_id_type=MESH,
        )

    def begin_hidden():
        for i in (2, 6, 4, 3, 7, 5, 1):
            for zsel in (1, 0):
                h_copy(i, zsel, me8).start()
        for zsel in range(2):
            h_got[zsel, :, me8] = h_v[dp_of(zsel, 0, 0)]
        acc[...] = jnp.zeros_like(acc)

    def spread_hidden():
        hidden_across.wait_recv()
        for i in range(1, 8):
            hf_copy(i, me8).start()
        h_far[:, me8] = h_cross[me8]

    def gradient(t, carry):
        for i in range(4):
            du_copy(t, 2 * i + 1 - c, 0, sibling).wait_recv()
        du = du_all[t].reshape(HALF * ROW, R)
        for zsel in (1, 0):
            acc[zsel] += lax.dot_general(
                h_got[zsel, t].reshape(HALF * ROW, BLK), du, TN,
                preferred_element_type=F32,
            )
        return carry

    def late_gradient(k):
        for i in range(4):
            du_copy(EARLY + k, 2 * i + 1 - c, 0, sibling).wait_recv()
        acc[0] += lax.dot_general(
            h_got[0, EARLY + k].reshape(HALF * ROW, BLK),
            du_all[EARLY + k].reshape(HALF * ROW, R), TN, preferred_element_type=F32,
        )

    def far_gradient(k):
        for i in range(4):
            far_copy(k, 2 * i + 1 - c, 0, sibling).wait_recv()
        acc[0] += lax.dot_general(
            h_far[k].reshape(HALF * ROW, BLK),
            du_far[k].reshape(HALF * ROW, R), TN, preferred_element_type=F32,
        )

    def z_copy(i):
        part = pl.ds(i * (BLK // PARTS), BLK // PARTS)
        return pltpu.make_async_remote_copy(
            src_ref=z_out.at[part], dst_ref=z_in.at[part],
            send_sem=z_send.at[i], recv_sem=z_recv.at[i],
            device_id=across, device_id_type=MESH,
        )

    def exchange(i):
        part = pl.ds(i * (BLK // PARTS), BLK // PARTS)
        z_out[part] = (acc[1, part] * SCALE).astype(BF16)
        z_copy(i).start()

    def late_stage(k):
        t = EARLY + k
        stage(t, True, t < STAGES - 2)
        cross_copy(k).start()
        for copy in rail(t):
            copy.start()

    def relayed(t, carry):
        for n in range(CHUNKS):
            relay_copy(t, n).wait_send()
        return carry

    def sent(t, carry):
        for copy in rail(t) + passed(t):
            copy.wait_send()
        return carry

    lax.fori_loop(0, 2, plain(False, True), 0)
    begin_hidden()
    lax.fori_loop(2, EARLY, plain(True, True), 0)
    late_stage(0)
    for t in range(EARLY):
        pass_rail(t)
    for i in range(1, 8):
        for zsel in range(2):
            h_copy(i, zsel, (me8 + 8 - i) % 8).wait_recv()
    lax.fori_loop(0, EARLY, gradient, 0)
    for i in range(BEFORE):
        exchange(i)
    spread_hidden()
    begin_far(0)
    late_stage(1)
    for i in range(BEFORE, PARTS):
        exchange(i)
    pass_rail(EARLY)
    pass_far(0)
    pass_rail(EARLY + 1)
    begin_far(1)
    for i in range(1, 8):
        hf_copy(i, (me8 + 8 - i) % 8).wait_recv()
    late_gradient(0)
    far_gradient(0)
    late_gradient(1)
    for copy in sends:
        copy.wait_send()
    lax.fori_loop(0, STAGES - 2, relayed, 0)
    lax.fori_loop(0, EARLY, sent, 0)
    for i in range(1, 8):
        hf_copy(i, me8).wait_send()
        for zsel in range(2):
            h_copy(i, zsel, me8).wait_send()
    hidden_across.wait_send()
    pass_far(1)
    far_gradient(1)

    for i in range(PARTS):
        part = pl.ds(i * (BLK // PARTS), BLK // PARTS)
        z_copy(i).wait_recv()
        grad_out[part] = acc[0, part] * SCALE + z_in[part].astype(F32)

    lax.fori_loop(EARLY, STAGES, sent, 0)
    for k in range(LATE):
        cross_copy(k).wait_send()
        for copy in far_rail(k) + far_passed(k):
            copy.wait_send()
    for i in range(PARTS):
        z_copy(i).wait_send()


def on_device(section_inputs, grad_first, value_master, first_moment, second_moment, output_weight):
    dma = pltpu.SemaphoreType.DMA
    grad = pl.pallas_call(
        lap_kernel,
        name="lap",
        out_shape=jax.ShapeDtypeStruct((BLK, R), F32),
        in_specs=[pl.BlockSpec(memory_space=pl.ANY)] * 4,
        out_specs=pl.BlockSpec(memory_space=pltpu.VMEM),
        scratch_shapes=[
            pltpu.VMEM((TOK, D), BF16),
            pltpu.VMEM((STAGES, CHUNKS, ROW, WIDE), BF16),
            pltpu.VMEM((BLK, R), F32),
            pltpu.VMEM((N_DP, BLK, R), BF16),
            pltpu.VMEM((N_DP, R, BLK), BF16),
            pltpu.VMEM((N_DP, STAGES, ROW, BLK), BF16),
            pltpu.VMEM((STAGES, ROW, 1), F32),
            pltpu.VMEM((STAGES, ROW, R), F32),
            pltpu.VMEM((STAGES, ROW, R), F32),
            pltpu.VMEM((2, ROW, R), F32),
            pltpu.VMEM((STAGES, HALF, ROW, R), BF16),
            pltpu.VMEM((LATE, HALF, ROW, R), BF16),
            pltpu.VMEM((2, STAGES, HALF, ROW, BLK), BF16),
            pltpu.VMEM((HALF, LATE, ROW, BLK), BF16),
            pltpu.VMEM((LATE, HALF, ROW, BLK), BF16),
            pltpu.VMEM((2, BLK, R), F32),
            pltpu.VMEM((BLK, R), BF16),
            pltpu.VMEM((BLK, R), BF16),
            pltpu.VMEM((6, CHUNKS, ROW, WIDE), BF16),
            dma((3 + 2 * CHUNKS,)),
            dma((64,)),
            dma((4, N_DP)),
            dma((6, CHUNKS)),
            dma((6, CHUNKS)),
            dma((8, 2)),
            dma((8, 2)),
            dma((STAGES, 8)),
            dma((STAGES, 8)),
            dma((LATE,)),
            dma((LATE,)),
            dma((LATE, 8)),
            dma((LATE, 8)),
            dma((8,)),
            dma((8,)),
            dma((PARTS,)),
            dma((PARTS,)),
        ],
        compiler_params=pltpu.CompilerParams(
            collective_id=0, has_side_effects=True, vmem_limit_bytes=60 * 1024 * 1024
        ),
        cost_estimate=pl.CostEstimate(flops=4 * 10**9, bytes_accessed=5 * 2**20, transcendentals=0),
    )(section_inputs, grad_first, value_master, output_weight)
    grad = grad[None]
    moment_a = 0.9 * first_moment.astype(F32) + 0.1 * grad
    moment_b = 0.95 * second_moment.astype(F32) + 0.05 * grad * grad
    master = value_master - 0.02 * (
        moment_a / (jnp.sqrt(moment_b) + 1e-08) + 0.1 * value_master
    )
    return master, moment_a.astype(BF16), moment_b.astype(BF16)


def solution(mesh):
    rows = P("section", "dp", None)
    return jax.shard_map(
        on_device,
        mesh=mesh,
        in_specs=(rows, rows, rows, rows, rows, P("section", None, "dp")),
        out_specs=(rows, rows, rows),
        check_vma=False,
    )
```

```python
import math

import jax
import jax.numpy as jnp
from jax import lax
from jax.experimental import pallas as pl
from jax.experimental.pallas import tpu as pltpu
from jax.sharding import PartitionSpec as P

MESH = pl.DeviceIdType.MESH
BF16 = jnp.bfloat16
F32 = jnp.float32

D = 4096
R = 512
TOK = 256
ROW = 32
STAGES = TOK // ROW
N_DP = 16
SECTIONS = 32
BLK = D // N_DP
CHUNKS = 4
WIDE = D // CHUNKS
PER = WIDE // BLK
HALF = 8
EARLY = 6
LATE = STAGES - EARLY
BEFORE = 1
PARTS = 4
SCALE = 1.0 / math.sqrt(D)

NT = (((1,), (1,)), ((), ()))
TN = (((0,), (0,)), ((), ()))


def lap_kernel(
    x_hbm, g_hbm, m_hbm, ow_hbm, grad_out,
    x_v, g_v, m_v, w_all, o_all, h_v, rinv_v, u_v, f_v, back_v,
    du_all, du_far, h_got, h_cross, h_far, acc, z_out, z_in, dx_v,
    local_sem, ag_send, ag_recv, relay_send, relay_recv, h_send, h_recv,
    du_send, du_recv, cross_send, cross_recv, far_send, far_recv, hf_send, hf_recv,
    z_send, z_recv,
):
    s = lax.axis_index("section")
    d = lax.axis_index("dp")
    zh, x, c = d // 8, (d // 2) % 4, d % 2
    me8 = d % 8

    def dp_of(zsel, dx, flip):
        z = zh if zsel == 0 else 1 - zh
        core = c if flip == 0 else 1 - c
        return z * 8 + ((x + dx + 4) % 4) * 2 + core

    def on_dp(zsel, dx, flip):
        return (s, dp_of(zsel, dx, flip))

    behind = ((s + SECTIONS - 1) % SECTIONS, d)
    ahead = ((s + 1) % SECTIONS, d)
    right, left = on_dp(0, 1, 0), on_dp(0, -1, 0)
    sibling, across = on_dp(0, 0, 1), on_dp(1, 0, 0)

    loads = {}

    def load(name, src, dst, at):
        loads[name] = pltpu.make_async_copy(src, dst, local_sem.at[at])
        loads[name].start()

    load("m", m_hbm.at[0], m_v, 0)
    load("ow", ow_hbm.at[0], o_all.at[d], 1)
    load("x", x_hbm.at[0], x_v, 2)
    for t in range(2):
        for n in range(CHUNKS):
            load(
                ("g", t, n),
                g_hbm.at[0, pl.ds(t * ROW, ROW), pl.ds(n * WIDE, WIDE)],
                g_v.at[t, n],
                3 + t * CHUNKS + n,
            )

    barrier = pltpu.get_barrier_semaphore()
    greet = [behind, ahead, across] + [(s, zh * 8 + (me8 + i) % 8) for i in range(1, 8)]
    for other in greet:
        pl.semaphore_signal(barrier, inc=1, device_id=other, device_id_type=MESH)

    loads["m"].wait()
    w_all[d] = m_v[...].astype(BF16)
    loads["ow"].wait()
    pl.semaphore_wait(barrier, len(greet))

    sends = []

    spans = ((0, 0, 128), (0, 128, 128), (1, 0, 256), (1, 256, 128), (1, 384, 128))
    rightward = (True, False, True, False, False)

    def piece(p, owner):
        weight, start, size = spans[p]
        return (o_all if weight else w_all).at[owner, pl.ds(start, size)]

    def pass_on(p, owner, target):
        copy = pltpu.make_async_remote_copy(
            src_ref=piece(p, owner), dst_ref=piece(p, owner),
            send_sem=ag_send.at[len(sends)], recv_sem=ag_recv.at[p, owner],
            device_id=target, device_id_type=MESH,
        )
        copy.start()
        sends.append(copy)

    def arrived(p, owner):
        pltpu.make_async_remote_copy(
            src_ref=piece(p, owner), dst_ref=piece(p, owner),
            send_sem=ag_send.at[0], recv_sem=ag_recv.at[p, owner],
            device_id=sibling, device_id_type=MESH,
        ).wait_recv()

    for p in range(5):
        for target in ((across,) if p < 2 else ()) + (right, left, sibling):
            pass_on(p, d, target)

    def handle(p, zsel, dx):
        owner = dp_of(zsel, dx, 0)
        arrived(p, owner)
        if dx == 0 or (dx == -1 and rightward[p]):
            pass_on(p, owner, right)
        if dx == 0 or (dx == 1 and not rightward[p]):
            pass_on(p, owner, left)
        pass_on(p, owner, sibling)

    def from_sibling(pieces, zsel):
        for p in pieces:
            for dx in (0, 1, -1, 2):
                arrived(p, dp_of(zsel, dx, 1))

    loads["x"].wait()

    def normalise(t, carry):
        xs = x_v[pl.ds(pl.multiple_of(t * ROW, ROW), ROW), :].astype(F32)
        rinv = lax.rsqrt(jnp.sum(xs * xs, axis=-1, keepdims=True) * (1.0 / D) + 1e-05)
        rinv_v[t] = rinv
        hidden = (xs * rinv).astype(BF16)
        for j in range(N_DP):
            h_v[j, t] = hidden[:, j * BLK : (j + 1) * BLK]
        return carry

    lax.fori_loop(0, STAGES, normalise, 0)
    u_v[...] = jnp.zeros_like(u_v)
    back_v[...] = jnp.zeros_like(back_v)
    for t in range(2):
        for n in range(CHUNKS):
            loads["g", t, n].wait()

    def upper(zsel, first=0, count=HALF):
        base = (zh if zsel == 0 else 1 - zh) * HALF

        def one(i, carry):
            j = base + i
            part = jnp.dot(
                h_v[j].reshape(TOK, BLK), w_all[j], preferred_element_type=F32
            )
            u_v[...] += part.reshape(STAGES, ROW, R)
            return carry

        lax.fori_loop(first, first + count, one, 0)

    def onto(total, grads, n):
        for i in range(PER):
            total = total + lax.dot_general(
                grads[:, i * BLK : (i + 1) * BLK], o_all[n * PER + i], NT,
                preferred_element_type=F32,
            )
        return total

    def first_back(zsel):
        base = (zh if zsel == 0 else 1 - zh) * (HALF // PER)

        def one(i, carry):
            n = base + i
            total = back_v[...].reshape(2 * ROW, R)
            grads = g_v[0:2, n].reshape(2 * ROW, WIDE)
            back_v[...] = onto(total, grads, n).reshape(2, ROW, R)
            return carry

        lax.fori_loop(0, HALF // PER, one, 0)

    hidden_across = pltpu.make_async_remote_copy(
        src_ref=h_v.at[pl.ds((1 - zh) * HALF, HALF), pl.ds(EARLY, LATE)], dst_ref=h_cross,
        send_sem=hf_send.at[0], recv_sem=hf_recv.at[0],
        device_id=across, device_id_type=MESH,
    )

    for event in (
        (0, 0, -1), (0, 0, 1), (1, 0, -1), (1, 0, 1), (0, 1, 0),
        (2, 0, -1), (2, 0, 1), (3, 0, -1), (3, 0, 1),
        (4, 0, -1), (4, 0, 1), (0, 0, 2), (1, 1, 0), (1, 0, 2),
    ):
        handle(*event)
        if event == (2, 0, -1):
            pass_on(2, d, across)
        if event == (1, 1, 0):
            pass_on(3, d, across)
            pass_on(4, d, across)
    from_sibling((0, 1), 0)
    upper(0)
    for event in (
        (2, 0, 2), (3, 0, 2), (4, 0, 2), (0, 1, -1), (0, 1, 1), (2, 1, 0),
        (1, 1, -1), (1, 1, 1), (0, 1, 2), (1, 1, 2),
    ):
        handle(*event)
    from_sibling((2, 3, 4), 0)
    first_back(0)
    for event in ((3, 1, 0), (2, 1, -1), (2, 1, 1), (4, 1, 0)):
        handle(*event)
    hidden_across.start()
    def gate(t, carry):
        u = u_v[t] * SCALE
        sig = jax.nn.sigmoid(u)
        u_v[t] = u
        f_v[t] = sig * (1.0 + u * (1.0 - sig))
        return carry

    from_sibling((0, 1), 1)
    for event in ((3, 1, -1), (3, 1, 1)):
        handle(*event)
    upper(1, 0, 4)
    for event in ((4, 1, -1), (4, 1, 1)):
        handle(*event)
    upper(1, 4, 4)
    for event in ((2, 1, 2), (3, 1, 2), (4, 1, 2)):
        handle(*event)
    lax.fori_loop(0, STAGES, gate, 0)
    from_sibling((2, 3, 4), 1)
    first_back(1)

    def relay_copy(t, n):
        return pltpu.make_async_remote_copy(
            src_ref=dx_v.at[t, n], dst_ref=g_v.at[t + 2, n],
            send_sem=relay_send.at[t, n], recv_sem=relay_recv.at[t, n],
            device_id=behind, device_id_type=MESH,
        )

    def mate(i):
        return (s, zh * 8 + (me8 + i) % 8)

    sib8 = 2 * x + 1 - c

    def du_copy(t, src, i, target):
        return pltpu.make_async_remote_copy(
            src_ref=du_all.at[t, src], dst_ref=du_all.at[t, src],
            send_sem=du_send.at[t, i], recv_sem=du_recv.at[t, src],
            device_id=target, device_id_type=MESH,
        )

    def rail(t):
        return [du_copy(t, me8, i, mate(2 * i)) for i in (1, 3, 2)] + [
            du_copy(t, me8, 0, sibling)
        ]

    def passed(t):
        return [du_copy(t, (me8 + 2 * i) % 8, 3 + i, sibling) for i in (1, 3, 2)]

    def pass_rail(t):
        for copy in passed(t):
            copy.wait_recv()
            copy.start()

    def cross_copy(k):
        return pltpu.make_async_remote_copy(
            src_ref=du_all.at[EARLY + k, me8], dst_ref=du_far.at[k, me8],
            send_sem=cross_send.at[k], recv_sem=cross_recv.at[k],
            device_id=across, device_id_type=MESH,
        )

    def far_copy(k, src, i, target):
        return pltpu.make_async_remote_copy(
            src_ref=du_far.at[k, src], dst_ref=du_far.at[k, src],
            send_sem=far_send.at[k, i], recv_sem=far_recv.at[k, src],
            device_id=target, device_id_type=MESH,
        )

    def far_rail(k):
        return [far_copy(k, me8, i, mate(2 * i)) for i in (1, 3, 2)] + [
            far_copy(k, me8, 0, sibling)
        ]

    def far_passed(k):
        return [far_copy(k, (me8 + 2 * i) % 8, 3 + i, sibling) for i in (1, 3, 2)]

    def begin_far(k):
        cross_copy(k).wait_recv()
        for copy in far_rail(k):
            copy.start()

    def pass_far(k):
        for copy in far_passed(k):
            copy.wait_recv()
            copy.start()

    def stage(t, arrives, leaves):
        if arrives:

            def take(n, total):
                relay_copy(t - 2, n).wait_recv()
                return onto(total, g_v[t, n], n)

            back = lax.fori_loop(0, CHUNKS, take, jnp.zeros((ROW, R), F32))
        else:
            back = back_v[t]
        du = (back * f_v[t]).astype(BF16)
        du_all[t, me8] = du
        if leaves:
            rinv = rinv_v[t]
            coef = jnp.sum(du.astype(F32) * u_v[t], axis=-1, keepdims=True) * (1.0 / D)
            coef = coef * rinv * rinv
            gain = rinv * SCALE
            rows = pl.ds(pl.multiple_of(t * ROW, ROW), ROW)

            def give(n, carry):
                wide = w_all[pl.ds(n * PER, PER)].reshape(WIDE, R)
                dh = lax.dot_general(du, wide, NT, preferred_element_type=F32)
                xs = x_v[rows, pl.ds(pl.multiple_of(n * WIDE, WIDE), WIDE)].astype(F32)
                dx = g_v[t, n].astype(F32) + gain * dh - xs * coef
                dx_v[t, n] = dx.astype(BF16)
                relay_copy(t, n).start()
                return carry

            lax.fori_loop(0, CHUNKS, give, 0)
        return du

    def plain(arrives, leaves):
        def one(t, carry):
            stage(t, arrives, leaves)
            for copy in rail(t):
                copy.start()
            return carry

        return one

    def h_copy(i, zsel, src):
        to = (me8 + i) % 8
        block = (zh if zsel == 0 else 1 - zh) * 8 + to
        count = STAGES if zsel == 0 else EARLY
        return pltpu.make_async_remote_copy(
            src_ref=h_v.at[block, pl.ds(0, count)], dst_ref=h_got.at[zsel, pl.ds(0, count), src],
            send_sem=h_send.at[i, zsel], recv_sem=h_recv.at[i, zsel],
            device_id=mate(i), device_id_type=MESH,
        )

    def hf_copy(i, src):
        return pltpu.make_async_remote_copy(
            src_ref=h_cross.at[(me8 + i) % 8], dst_ref=h_far.at[:, src],
            send_sem=hf_send.at[i], recv_sem=hf_recv.at[i],
            device_id=mate(i), device_id_type=MESH,
        )

    def begin_hidden():
        for i in (2, 6, 4, 3, 7, 5, 1):
            for zsel in (1, 0):
                h_copy(i, zsel, me8).start()
        for zsel in range(2):
            h_got[zsel, :, me8] = h_v[dp_of(zsel, 0, 0)]
        acc[...] = jnp.zeros_like(acc)

    def spread_hidden():
        hidden_across.wait_recv()
        for i in range(1, 8):
            hf_copy(i, me8).start()
        h_far[:, me8] = h_cross[me8]

    def gradient(t, carry):
        for i in range(4):
            du_copy(t, 2 * i + 1 - c, 0, sibling).wait_recv()
        du = du_all[t].reshape(HALF * ROW, R)
        for zsel in (1, 0):
            acc[zsel] += lax.dot_general(
                h_got[zsel, t].reshape(HALF * ROW, BLK), du, TN,
                preferred_element_type=F32,
            )
        return carry

    def late_gradient(k):
        for i in range(4):
            du_copy(EARLY + k, 2 * i + 1 - c, 0, sibling).wait_recv()
        acc[0] += lax.dot_general(
            h_got[0, EARLY + k].reshape(HALF * ROW, BLK),
            du_all[EARLY + k].reshape(HALF * ROW, R), TN, preferred_element_type=F32,
        )

    def far_gradient(k):
        for i in range(4):
            far_copy(k, 2 * i + 1 - c, 0, sibling).wait_recv()
        acc[0] += lax.dot_general(
            h_far[k].reshape(HALF * ROW, BLK),
            du_far[k].reshape(HALF * ROW, R), TN, preferred_element_type=F32,
        )

    def z_copy(i):
        part = pl.ds(i * (BLK // PARTS), BLK // PARTS)
        return pltpu.make_async_remote_copy(
            src_ref=z_out.at[part], dst_ref=z_in.at[part],
            send_sem=z_send.at[i], recv_sem=z_recv.at[i],
            device_id=across, device_id_type=MESH,
        )

    def exchange(i):
        part = pl.ds(i * (BLK // PARTS), BLK // PARTS)
        z_out[part] = (acc[1, part] * SCALE).astype(BF16)
        z_copy(i).start()

    def late_stage(k):
        t = EARLY + k
        stage(t, True, t < STAGES - 2)
        cross_copy(k).start()
        for copy in rail(t):
            copy.start()

    def relayed(t, carry):
        for n in range(CHUNKS):
            relay_copy(t, n).wait_send()
        return carry

    def sent(t, carry):
        for copy in rail(t) + passed(t):
            copy.wait_send()
        return carry

    lax.fori_loop(0, 2, plain(False, True), 0)
    begin_hidden()
    lax.fori_loop(2, EARLY, plain(True, True), 0)
    late_stage(0)
    for t in range(EARLY):
        pass_rail(t)
    for i in range(1, 8):
        for zsel in range(2):
            h_copy(i, zsel, (me8 + 8 - i) % 8).wait_recv()
    lax.fori_loop(0, EARLY, gradient, 0)
    for i in range(BEFORE):
        exchange(i)
    spread_hidden()
    late_stage(1)
    for i in range(BEFORE, PARTS):
        exchange(i)
    begin_far(0)
    pass_rail(EARLY)
    pass_rail(EARLY + 1)
    begin_far(1)
    pass_far(0)
    for i in range(1, 8):
        hf_copy(i, (me8 + 8 - i) % 8).wait_recv()
    late_gradient(0)
    far_gradient(0)
    late_gradient(1)
    for copy in sends:
        copy.wait_send()
    lax.fori_loop(0, STAGES - 2, relayed, 0)
    lax.fori_loop(0, EARLY, sent, 0)
    for i in range(1, 8):
        hf_copy(i, me8).wait_send()
        for zsel in range(2):
            h_copy(i, zsel, me8).wait_send()
    hidden_across.wait_send()
    pass_far(1)
    far_gradient(1)

    for i in range(PARTS):
        part = pl.ds(i * (BLK // PARTS), BLK // PARTS)
        z_copy(i).wait_recv()
        grad_out[part] = acc[0, part] * SCALE + z_in[part].astype(F32)

    lax.fori_loop(EARLY, STAGES, sent, 0)
    for k in range(LATE):
        cross_copy(k).wait_send()
        for copy in far_rail(k) + far_passed(k):
            copy.wait_send()
    for i in range(PARTS):
        z_copy(i).wait_send()


def on_device(section_inputs, grad_first, value_master, first_moment, second_moment, output_weight):
    dma = pltpu.SemaphoreType.DMA
    grad = pl.pallas_call(
        lap_kernel,
        name="lap",
        out_shape=jax.ShapeDtypeStruct((BLK, R), F32),
        in_specs=[pl.BlockSpec(memory_space=pl.ANY)] * 4,
        out_specs=pl.BlockSpec(memory_space=pltpu.VMEM),
        scratch_shapes=[
            pltpu.VMEM((TOK, D), BF16),
            pltpu.VMEM((STAGES, CHUNKS, ROW, WIDE), BF16),
            pltpu.VMEM((BLK, R), F32),
            pltpu.VMEM((N_DP, BLK, R), BF16),
            pltpu.VMEM((N_DP, R, BLK), BF16),
            pltpu.VMEM((N_DP, STAGES, ROW, BLK), BF16),
            pltpu.VMEM((STAGES, ROW, 1), F32),
            pltpu.VMEM((STAGES, ROW, R), F32),
            pltpu.VMEM((STAGES, ROW, R), F32),
            pltpu.VMEM((2, ROW, R), F32),
            pltpu.VMEM((STAGES, HALF, ROW, R), BF16),
            pltpu.VMEM((LATE, HALF, ROW, R), BF16),
            pltpu.VMEM((2, STAGES, HALF, ROW, BLK), BF16),
            pltpu.VMEM((HALF, LATE, ROW, BLK), BF16),
            pltpu.VMEM((LATE, HALF, ROW, BLK), BF16),
            pltpu.VMEM((2, BLK, R), F32),
            pltpu.VMEM((BLK, R), BF16),
            pltpu.VMEM((BLK, R), BF16),
            pltpu.VMEM((6, CHUNKS, ROW, WIDE), BF16),
            dma((3 + 2 * CHUNKS,)),
            dma((80,)),
            dma((5, N_DP)),
            dma((6, CHUNKS)),
            dma((6, CHUNKS)),
            dma((8, 2)),
            dma((8, 2)),
            dma((STAGES, 8)),
            dma((STAGES, 8)),
            dma((LATE,)),
            dma((LATE,)),
            dma((LATE, 8)),
            dma((LATE, 8)),
            dma((8,)),
            dma((8,)),
            dma((PARTS,)),
            dma((PARTS,)),
        ],
        compiler_params=pltpu.CompilerParams(
            collective_id=0, has_side_effects=True, vmem_limit_bytes=60 * 1024 * 1024
        ),
        cost_estimate=pl.CostEstimate(flops=4 * 10**9, bytes_accessed=5 * 2**20, transcendentals=0),
    )(section_inputs, grad_first, value_master, output_weight)
    grad = grad[None]
    moment_a = 0.9 * first_moment.astype(F32) + 0.1 * grad
    moment_b = 0.95 * second_moment.astype(F32) + 0.05 * grad * grad
    master = value_master - 0.02 * (
        moment_a / (jnp.sqrt(moment_b) + 1e-08) + 0.1 * value_master
    )
    return master, moment_a.astype(BF16), moment_b.astype(BF16)


def solution(mesh):
    rows = P("section", "dp", None)
    return jax.shard_map(
        on_device,
        mesh=mesh,
        in_specs=(rows, rows, rows, rows, rows, P("section", None, "dp")),
        out_specs=(rows, rows, rows),
        check_vma=False,
    )
```

```python
import math

import jax
import jax.numpy as jnp
from jax import lax
from jax.experimental import pallas as pl
from jax.experimental.pallas import tpu as pltpu
from jax.sharding import PartitionSpec as P

MESH = pl.DeviceIdType.MESH
BF16 = jnp.bfloat16
F32 = jnp.float32

D = 4096
R = 512
TOK = 256
ROW = 32
STAGES = TOK // ROW
N_DP = 16
SECTIONS = 32
BLK = D // N_DP
CHUNKS = 4
WIDE = D // CHUNKS
PER = WIDE // BLK
HALF = 8
EARLY = 6
LATE = STAGES - EARLY
BEFORE = 1
PARTS = 4
SCALE = 1.0 / math.sqrt(D)

NT = (((1,), (1,)), ((), ()))
TN = (((0,), (0,)), ((), ()))


def lap_kernel(
    x_hbm, g_hbm, m_hbm, ow_hbm, grad_out,
    x_v, g_v, m_v, w_all, o_all, h_v, rinv_v, u_v, f_v, back_v,
    du_all, du_far, h_got, h_cross, h_far, acc, z_out, z_in, dx_v,
    local_sem, ag_send, ag_recv, relay_send, relay_recv, h_send, h_recv,
    du_send, du_recv, cross_send, cross_recv, far_send, far_recv, hf_send, hf_recv,
    z_send, z_recv,
):
    s = lax.axis_index("section")
    d = lax.axis_index("dp")
    zh, x, c = d // 8, (d // 2) % 4, d % 2
    me8 = d % 8

    def dp_of(zsel, dx, flip):
        z = zh if zsel == 0 else 1 - zh
        core = c if flip == 0 else 1 - c
        return z * 8 + ((x + dx + 4) % 4) * 2 + core

    def on_dp(zsel, dx, flip):
        return (s, dp_of(zsel, dx, flip))

    behind = ((s + SECTIONS - 1) % SECTIONS, d)
    ahead = ((s + 1) % SECTIONS, d)
    right, left = on_dp(0, 1, 0), on_dp(0, -1, 0)
    sibling, across = on_dp(0, 0, 1), on_dp(1, 0, 0)

    loads = {}

    def load(name, src, dst, at):
        loads[name] = pltpu.make_async_copy(src, dst, local_sem.at[at])
        loads[name].start()

    load("m", m_hbm.at[0], m_v, 0)
    load("ow", ow_hbm.at[0], o_all.at[d], 1)
    load("x", x_hbm.at[0], x_v, 2)
    for t in range(2):
        for n in range(CHUNKS):
            load(
                ("g", t, n),
                g_hbm.at[0, pl.ds(t * ROW, ROW), pl.ds(n * WIDE, WIDE)],
                g_v.at[t, n],
                3 + t * CHUNKS + n,
            )

    barrier = pltpu.get_barrier_semaphore()
    greet = [behind, ahead, across] + [(s, zh * 8 + (me8 + i) % 8) for i in range(1, 8)]
    for other in greet:
        pl.semaphore_signal(barrier, inc=1, device_id=other, device_id_type=MESH)

    loads["m"].wait()
    w_all[d] = m_v[...].astype(BF16)
    loads["ow"].wait()
    pl.semaphore_wait(barrier, len(greet))

    sends = []

    spans = ((0, 0, 128), (0, 128, 128), (1, 0, 256), (1, 256, 128), (1, 384, 128))
    rightward = (True, False, True, False, False)

    def piece(p, owner):
        weight, start, size = spans[p]
        return (o_all if weight else w_all).at[owner, pl.ds(start, size)]

    def pass_on(p, owner, target, now=True):
        copy = pltpu.make_async_remote_copy(
            src_ref=piece(p, owner), dst_ref=piece(p, owner),
            send_sem=ag_send.at[len(sends)], recv_sem=ag_recv.at[p, owner],
            device_id=target, device_id_type=MESH,
        )
        sends.append(copy)
        if now:
            copy.start()
        return copy

    def arrived(p, owner):
        pltpu.make_async_remote_copy(
            src_ref=piece(p, owner), dst_ref=piece(p, owner),
            send_sem=ag_send.at[0], recv_sem=ag_recv.at[p, owner],
            device_id=sibling, device_id_type=MESH,
        ).wait_recv()

    for p in range(5):
        for target in ((across,) if p < 2 else ()) + (right, left, sibling):
            pass_on(p, d, target)

    def handle(p, zsel, dx):
        owner = dp_of(zsel, dx, 0)
        arrived(p, owner)
        if dx == 0 or (dx == -1 and rightward[p]):
            pass_on(p, owner, right)
        if dx == 0 or (dx == 1 and not rightward[p]):
            pass_on(p, owner, left)
        pass_on(p, owner, sibling)

    def from_sibling(pieces, zsel):
        for p in pieces:
            for dx in (0, 1, -1, 2):
                arrived(p, dp_of(zsel, dx, 1))

    loads["x"].wait()

    def normalise(t, carry):
        xs = x_v[pl.ds(pl.multiple_of(t * ROW, ROW), ROW), :].astype(F32)
        rinv = lax.rsqrt(jnp.sum(xs * xs, axis=-1, keepdims=True) * (1.0 / D) + 1e-05)
        rinv_v[t] = rinv
        hidden = (xs * rinv).astype(BF16)
        for j in range(N_DP):
            h_v[j, t] = hidden[:, j * BLK : (j + 1) * BLK]
        return carry

    lax.fori_loop(0, STAGES, normalise, 0)
    u_v[...] = jnp.zeros_like(u_v)
    back_v[...] = jnp.zeros_like(back_v)
    for t in range(2):
        for n in range(CHUNKS):
            loads["g", t, n].wait()

    def upper(zsel, first=0, count=HALF):
        base = (zh if zsel == 0 else 1 - zh) * HALF

        def one(i, carry):
            j = base + i
            part = jnp.dot(
                h_v[j].reshape(TOK, BLK), w_all[j], preferred_element_type=F32
            )
            u_v[...] += part.reshape(STAGES, ROW, R)
            return carry

        lax.fori_loop(first, first + count, one, 0)

    def onto(total, grads, n):
        for i in range(PER):
            total = total + lax.dot_general(
                grads[:, i * BLK : (i + 1) * BLK], o_all[n * PER + i], NT,
                preferred_element_type=F32,
            )
        return total

    def first_back(zsel):
        base = (zh if zsel == 0 else 1 - zh) * (HALF // PER)

        def one(i, carry):
            n = base + i
            total = back_v[...].reshape(2 * ROW, R)
            grads = g_v[0:2, n].reshape(2 * ROW, WIDE)
            back_v[...] = onto(total, grads, n).reshape(2, ROW, R)
            return carry

        lax.fori_loop(0, HALF // PER, one, 0)

    hidden_across = pltpu.make_async_remote_copy(
        src_ref=h_v.at[pl.ds((1 - zh) * HALF, HALF), pl.ds(EARLY, LATE)], dst_ref=h_cross,
        send_sem=hf_send.at[0], recv_sem=hf_recv.at[0],
        device_id=across, device_id_type=MESH,
    )

    for event in (
        (0, 0, -1), (0, 0, 1), (1, 0, -1), (1, 0, 1), (0, 1, 0),
        (2, 0, -1), (2, 0, 1), (3, 0, -1), (3, 0, 1),
        (4, 0, -1), (4, 0, 1), (0, 0, 2), (1, 1, 0), (1, 0, 2),
    ):
        handle(*event)
        if event == (1, 0, 1):
            held = pass_on(2, d, across, False)
            pl.when(s % 8 != 0)(held.start)
        if event == (2, 0, -1):
            pl.when(s % 8 == 0)(held.start)
        if event == (1, 1, 0):
            pass_on(3, d, across)
            pass_on(4, d, across)
    from_sibling((0, 1), 0)
    upper(0)
    for event in (
        (2, 0, 2), (3, 0, 2), (4, 0, 2), (0, 1, -1), (0, 1, 1), (2, 1, 0),
        (1, 1, -1), (1, 1, 1), (0, 1, 2), (1, 1, 2),
    ):
        handle(*event)
    from_sibling((2, 3, 4), 0)
    first_back(0)
    for event in ((3, 1, 0), (2, 1, -1), (2, 1, 1), (4, 1, 0)):
        handle(*event)
    hidden_across.start()
    def gate(t, carry):
        u = u_v[t] * SCALE
        sig = jax.nn.sigmoid(u)
        u_v[t] = u
        f_v[t] = sig * (1.0 + u * (1.0 - sig))
        return carry

    from_sibling((0, 1), 1)
    for event in ((3, 1, -1), (3, 1, 1)):
        handle(*event)
    upper(1, 0, 4)
    for event in ((4, 1, -1), (4, 1, 1)):
        handle(*event)
    upper(1, 4, 4)
    for event in ((2, 1, 2), (3, 1, 2), (4, 1, 2)):
        handle(*event)
    lax.fori_loop(0, STAGES, gate, 0)
    from_sibling((2, 3, 4), 1)
    first_back(1)

    def relay_copy(t, n):
        return pltpu.make_async_remote_copy(
            src_ref=dx_v.at[t, n], dst_ref=g_v.at[t + 2, n],
            send_sem=relay_send.at[t, n], recv_sem=relay_recv.at[t, n],
            device_id=behind, device_id_type=MESH,
        )

    def mate(i):
        return (s, zh * 8 + (me8 + i) % 8)

    sib8 = 2 * x + 1 - c

    def du_copy(t, src, i, target):
        return pltpu.make_async_remote_copy(
            src_ref=du_all.at[t, src], dst_ref=du_all.at[t, src],
            send_sem=du_send.at[t, i], recv_sem=du_recv.at[t, src],
            device_id=target, device_id_type=MESH,
        )

    def rail(t):
        return [du_copy(t, me8, i, mate(2 * i)) for i in (1, 3, 2)] + [
            du_copy(t, me8, 0, sibling)
        ]

    def passed(t):
        return [du_copy(t, (me8 + 2 * i) % 8, 3 + i, sibling) for i in (1, 3, 2)]

    def pass_rail(t):
        for copy in passed(t):
            copy.wait_recv()
            copy.start()

    def cross_copy(k):
        return pltpu.make_async_remote_copy(
            src_ref=du_all.at[EARLY + k, me8], dst_ref=du_far.at[k, me8],
            send_sem=cross_send.at[k], recv_sem=cross_recv.at[k],
            device_id=across, device_id_type=MESH,
        )

    def far_copy(k, src, i, target):
        return pltpu.make_async_remote_copy(
            src_ref=du_far.at[k, src], dst_ref=du_far.at[k, src],
            send_sem=far_send.at[k, i], recv_sem=far_recv.at[k, src],
            device_id=target, device_id_type=MESH,
        )

    def far_rail(k):
        if k == LATE - 1:
            return [far_copy(k, me8, i, mate(i)) for i in (2, 6, 4, 3, 7, 5, 1)]
        return [far_copy(k, me8, i, mate(2 * i)) for i in (1, 3, 2)] + [
            far_copy(k, me8, 0, sibling)
        ]

    def far_passed(k):
        if k == LATE - 1:
            return []
        return [far_copy(k, (me8 + 2 * i) % 8, 3 + i, sibling) for i in (1, 3, 2)]

    def begin_far(k):
        cross_copy(k).wait_recv()
        for copy in far_rail(k):
            copy.start()

    def pass_far(k):
        for copy in far_passed(k):
            copy.wait_recv()
            copy.start()

    def stage(t, arrives, leaves):
        if arrives:

            def take(n, total):
                relay_copy(t - 2, n).wait_recv()
                return onto(total, g_v[t, n], n)

            back = lax.fori_loop(0, CHUNKS, take, jnp.zeros((ROW, R), F32))
        else:
            back = back_v[t]
        du = (back * f_v[t]).astype(BF16)
        du_all[t, me8] = du
        if leaves:
            rinv = rinv_v[t]
            coef = jnp.sum(du.astype(F32) * u_v[t], axis=-1, keepdims=True) * (1.0 / D)
            coef = coef * rinv * rinv
            gain = rinv * SCALE
            rows = pl.ds(pl.multiple_of(t * ROW, ROW), ROW)

            def give(n, carry):
                wide = w_all[pl.ds(n * PER, PER)].reshape(WIDE, R)
                dh = lax.dot_general(du, wide, NT, preferred_element_type=F32)
                xs = x_v[rows, pl.ds(pl.multiple_of(n * WIDE, WIDE), WIDE)].astype(F32)
                dx = g_v[t, n].astype(F32) + gain * dh - xs * coef
                dx_v[t, n] = dx.astype(BF16)
                relay_copy(t, n).start()
                return carry

            lax.fori_loop(0, CHUNKS, give, 0)
        return du

    def plain(arrives, leaves):
        def one(t, carry):
            stage(t, arrives, leaves)
            for copy in rail(t):
                copy.start()
            return carry

        return one

    def h_copy(i, zsel, src):
        to = (me8 + i) % 8
        block = (zh if zsel == 0 else 1 - zh) * 8 + to
        count = STAGES if zsel == 0 else EARLY
        return pltpu.make_async_remote_copy(
            src_ref=h_v.at[block, pl.ds(0, count)], dst_ref=h_got.at[zsel, pl.ds(0, count), src],
            send_sem=h_send.at[i, zsel], recv_sem=h_recv.at[i, zsel],
            device_id=mate(i), device_id_type=MESH,
        )

    def hf_copy(i, src):
        return pltpu.make_async_remote_copy(
            src_ref=h_cross.at[(me8 + i) % 8], dst_ref=h_far.at[:, src],
            send_sem=hf_send.at[i], recv_sem=hf_recv.at[i],
            device_id=mate(i), device_id_type=MESH,
        )

    def begin_hidden():
        for i in (2, 6, 4, 3, 7, 5, 1):
            for zsel in (1, 0):
                h_copy(i, zsel, me8).start()
        for zsel in range(2):
            h_got[zsel, :, me8] = h_v[dp_of(zsel, 0, 0)]
        acc[...] = jnp.zeros_like(acc)

    def spread_hidden():
        hidden_across.wait_recv()
        for i in range(1, 8):
            hf_copy(i, me8).start()
        h_far[:, me8] = h_cross[me8]

    def gradient(t, carry):
        for i in range(4):
            du_copy(t, 2 * i + 1 - c, 0, sibling).wait_recv()
        du = du_all[t].reshape(HALF * ROW, R)
        for zsel in (1, 0):
            acc[zsel] += lax.dot_general(
                h_got[zsel, t].reshape(HALF * ROW, BLK), du, TN,
                preferred_element_type=F32,
            )
        return carry

    def late_gradient(k):
        for i in range(4):
            du_copy(EARLY + k, 2 * i + 1 - c, 0, sibling).wait_recv()
        acc[0] += lax.dot_general(
            h_got[0, EARLY + k].reshape(HALF * ROW, BLK),
            du_all[EARLY + k].reshape(HALF * ROW, R), TN, preferred_element_type=F32,
        )

    def far_gradient(k):
        if k == LATE - 1:
            sources = [(me8 + i) % 8 for i in range(1, 8)]
        else:
            sources = [2 * i + 1 - c for i in range(4)]
        for src in sources:
            far_copy(k, src, 0, sibling).wait_recv()
        acc[0] += lax.dot_general(
            h_far[k].reshape(HALF * ROW, BLK),
            du_far[k].reshape(HALF * ROW, R), TN, preferred_element_type=F32,
        )

    def z_copy(i):
        part = pl.ds(i * (BLK // PARTS), BLK // PARTS)
        return pltpu.make_async_remote_copy(
            src_ref=z_out.at[part], dst_ref=z_in.at[part],
            send_sem=z_send.at[i], recv_sem=z_recv.at[i],
            device_id=across, device_id_type=MESH,
        )

    def exchange(i):
        part = pl.ds(i * (BLK // PARTS), BLK // PARTS)
        z_out[part] = (acc[1, part] * SCALE).astype(BF16)
        z_copy(i).start()

    def late_stage(k):
        t = EARLY + k
        stage(t, True, t < STAGES - 2)
        cross_copy(k).start()
        for copy in rail(t):
            copy.start()

    def relayed(t, carry):
        for n in range(CHUNKS):
            relay_copy(t, n).wait_send()
        return carry

    def sent(t, carry):
        for copy in rail(t) + passed(t):
            copy.wait_send()
        return carry

    lax.fori_loop(0, 2, plain(False, True), 0)
    begin_hidden()
    lax.fori_loop(2, EARLY, plain(True, True), 0)
    late_stage(0)
    for t in range(EARLY):
        pass_rail(t)
    for i in range(1, 8):
        for zsel in range(2):
            h_copy(i, zsel, (me8 + 8 - i) % 8).wait_recv()
    lax.fori_loop(0, EARLY, gradient, 0)
    for i in range(BEFORE):
        exchange(i)
    spread_hidden()
    late_stage(1)
    for i in range(BEFORE, PARTS):
        exchange(i)
    begin_far(0)
    pass_rail(EARLY)
    pass_rail(EARLY + 1)
    begin_far(1)
    pass_far(0)
    for i in range(1, 8):
        hf_copy(i, (me8 + 8 - i) % 8).wait_recv()
    late_gradient(0)
    far_gradient(0)
    late_gradient(1)
    for copy in sends:
        copy.wait_send()
    lax.fori_loop(0, STAGES - 2, relayed, 0)
    lax.fori_loop(0, EARLY, sent, 0)
    for i in range(1, 8):
        hf_copy(i, me8).wait_send()
        for zsel in range(2):
            h_copy(i, zsel, me8).wait_send()
    hidden_across.wait_send()
    far_gradient(1)

    lax.fori_loop(EARLY, STAGES, sent, 0)
    for k in range(LATE):
        cross_copy(k).wait_send()
        for copy in far_rail(k) + far_passed(k):
            copy.wait_send()
    for i in range(PARTS):
        part = pl.ds(i * (BLK // PARTS), BLK // PARTS)
        z_copy(i).wait_recv()
        grad_out[part] = acc[0, part] * SCALE + z_in[part].astype(F32)

    for i in range(PARTS):
        z_copy(i).wait_send()


def on_device(section_inputs, grad_first, value_master, first_moment, second_moment, output_weight):
    dma = pltpu.SemaphoreType.DMA
    grad = pl.pallas_call(
        lap_kernel,
        name="lap",
        out_shape=jax.ShapeDtypeStruct((BLK, R), F32),
        in_specs=[pl.BlockSpec(memory_space=pl.ANY)] * 4,
        out_specs=pl.BlockSpec(memory_space=pltpu.VMEM),
        scratch_shapes=[
            pltpu.VMEM((TOK, D), BF16),
            pltpu.VMEM((STAGES, CHUNKS, ROW, WIDE), BF16),
            pltpu.VMEM((BLK, R), F32),
            pltpu.VMEM((N_DP, BLK, R), BF16),
            pltpu.VMEM((N_DP, R, BLK), BF16),
            pltpu.VMEM((N_DP, STAGES, ROW, BLK), BF16),
            pltpu.VMEM((STAGES, ROW, 1), F32),
            pltpu.VMEM((STAGES, ROW, R), F32),
            pltpu.VMEM((STAGES, ROW, R), F32),
            pltpu.VMEM((2, ROW, R), F32),
            pltpu.VMEM((STAGES, HALF, ROW, R), BF16),
            pltpu.VMEM((LATE, HALF, ROW, R), BF16),
            pltpu.VMEM((2, STAGES, HALF, ROW, BLK), BF16),
            pltpu.VMEM((HALF, LATE, ROW, BLK), BF16),
            pltpu.VMEM((LATE, HALF, ROW, BLK), BF16),
            pltpu.VMEM((2, BLK, R), F32),
            pltpu.VMEM((BLK, R), BF16),
            pltpu.VMEM((BLK, R), BF16),
            pltpu.VMEM((6, CHUNKS, ROW, WIDE), BF16),
            dma((3 + 2 * CHUNKS,)),
            dma((80,)),
            dma((5, N_DP)),
            dma((6, CHUNKS)),
            dma((6, CHUNKS)),
            dma((8, 2)),
            dma((8, 2)),
            dma((STAGES, 8)),
            dma((STAGES, 8)),
            dma((LATE,)),
            dma((LATE,)),
            dma((LATE, 8)),
            dma((LATE, 8)),
            dma((8,)),
            dma((8,)),
            dma((PARTS,)),
            dma((PARTS,)),
        ],
        compiler_params=pltpu.CompilerParams(
            collective_id=0, has_side_effects=True, vmem_limit_bytes=60 * 1024 * 1024
        ),
        cost_estimate=pl.CostEstimate(flops=4 * 10**9, bytes_accessed=5 * 2**20, transcendentals=0),
    )(section_inputs, grad_first, value_master, output_weight)
    grad = grad[None]
    moment_a = 0.9 * first_moment.astype(F32) + 0.1 * grad
    moment_b = 0.95 * second_moment.astype(F32) + 0.05 * grad * grad
    master = value_master - 0.02 * (
        moment_a / (jnp.sqrt(moment_b) + 1e-08) + 0.1 * value_master
    )
    return master, moment_a.astype(BF16), moment_b.astype(BF16)


def solution(mesh):
    rows = P("section", "dp", None)
    return jax.shard_map(
        on_device,
        mesh=mesh,
        in_specs=(rows, rows, rows, rows, rows, P("section", None, "dp")),
        out_specs=(rows, rows, rows),
        check_vma=False,
    )
```
